128 devices in a mesh: crow: 8 (over x, z_hi), ccol: 4 (over z_lo, core), band: 4 (over y).
Axes of the slice: x: 4, y: 4, z: 4 (z_hi: 2, z_lo: 2; z = z_hi * 2 + z_lo), core: 2. Of those that a mesh axis runs over, the one named last changes fastest.
Arguments:
- light_field: bfloat16 [4, 16, 16, 64, 4096], P(None, 'crow', 'ccol', 'band'), may hold values from -6 to 6
- channel_weights: float32 [4], replicated, may hold values from 0.2 to 1
Outputs:
- depth: float32 [16, 16, 64, 4096], P('crow', 'ccol', 'band')
The draws below stay inside these ranges and needn't reach their ends.
All inputs are finite; a program needn't handle non-finite values.
Results may differ from the reference program's by a relative error of at most 0.0043.
Values may be sent and summed in bfloat16 or wider, within the bound.
No kernel may reach another device: no remote copies, remote signals or barrier semaphores. Data moves between devices by JAX's collectives and lax.ppermute only.
A program may use at most 128 MiB of HBM per device.

```python
import jax
import jax.numpy as jnp
from jax import lax

C = 4
S = 16
T_SIZE = 16
U = 4096
V = 64


def block_scale(key, shape, cuts, low, high):
    def one(dim, shards_of):
        heights = jax.random.uniform(jax.random.fold_in(jax.random.fold_in(key, 6), dim), (shards_of,), jnp.float32, low / len(cuts), high / len(cuts))
        return jnp.repeat(jnp.exp(heights), shape[dim] // shards_of).reshape((-1,) + (1,) * (len(shape) - dim - 1))

    factor_of = one(*cuts[0])
    for cut in cuts[1:]:
        factor_of = factor_of * one(*cut)
    return factor_of


def noise(key, dims, scale, most, split=(), dtype=jnp.bfloat16):
    entries = scale * jax.random.normal(key, dims, jnp.float32)
    if split:
        entries = entries * block_scale(key, dims, split, -0.22, 0.18)
    return jnp.clip(entries, -most, most).astype(dtype)


def setup_inputs(seed: int = 0) -> dict:
    key_of = jax.random.split(jax.random.key(seed), 3)
    return {
        "light_field": noise(key_of[0], (C, S, T_SIZE, V, U), 1.0, 6.0, ((1, 8), (2, 4), (3, 4))),
        "channel_weights": jnp.clip(jax.random.uniform(key_of[1], (C,), jnp.float32, 0.2, 1.0), 0.2, 1.0),
    }


def neighbour(field, axis, offset):
    length = field.shape[axis]
    reach = abs(offset)
    widths = [(0, 0)] * field.ndim
    widths[axis] = (reach, reach)
    padded = jnp.pad(field, widths)
    return lax.slice_in_dim(padded, reach + offset, reach + offset + length, axis=axis)


def gradient(field, axis):
    return 0.5 * (neighbour(field, axis, 1) - neighbour(field, axis, -1))


def smooth(field, axis):
    near = neighbour(field, axis, 1) + neighbour(field, axis, -1)
    far_terms = neighbour(field, axis, 2) + neighbour(field, axis, -2)
    return (6.0 * field + 4.0 * near + far_terms) / 16.0


def epi_tensor(gray_level, cam_axis, img_axis, row_mask):
    field = gray_level.astype(jnp.float32)
    grad_cam = gradient(field, cam_axis) * row_mask
    grad_img = gradient(field, img_axis) * row_mask

    def both(values):
        return smooth(smooth(values, cam_axis), img_axis)

    jaa = both(grad_cam * grad_cam)
    jab = both(grad_cam * grad_img)
    jbb = both(grad_img * grad_img)
    slope = -jab / (jbb + 0.1)
    spread = jaa - jbb
    total = jaa + jbb
    confidence = (spread * spread + 4.0 * jab * jab) / (total * total + 0.1)
    return slope, confidence


def combine_depth(slope_h, conf_h, slope_v, conf_v):
    return (conf_h * slope_h + conf_v * slope_v) / (conf_h + conf_v + 0.1)


def reference(light_field, channel_weights):
    summed = light_field[0].astype(jnp.float32) * channel_weights[0]
    for channel in range(1, C):
        summed = summed + light_field[channel].astype(jnp.float32) * channel_weights[channel]
    gray_level = summed.astype(jnp.bfloat16)
    slope_h, conf_h = lax.map(lambda camera_slab: epi_tensor(camera_slab, 0, 2, 1.0), gray_level)
    slope_v, conf_v = lax.map(lambda camera_slab: epi_tensor(camera_slab, 0, 1, 1.0), jnp.swapaxes(gray_level, 0, 1))
    slope_v = jnp.swapaxes(slope_v, 0, 1)
    conf_v = jnp.swapaxes(conf_v, 0, 1)
    return combine_depth(slope_h, conf_h, slope_v, conf_v)
```

```python
import functools

import jax
import jax.numpy as jnp
from jax import lax
from jax.experimental import pallas as pl
from jax.experimental.pallas import tpu as pltpu
from jax.sharding import PartitionSpec as P

F32, BF16 = jnp.float32, jnp.bfloat16
LANES = 128
MIB = 1 << 20
NT = (((1,), (1,)), ((), ()))


def iota(shape, dim):
    return lax.broadcasted_iota(jnp.int32, shape, dim)


def ones_where(*conditions_and_values):
    total = None
    for condition, value in conditions_and_values:
        term = jnp.where(condition, F32(value), F32(0.0))
        total = term if total is None else total + term
    return total


def cascade(values):
    for _ in range(4):
        values = values[:-1] + values[1:]
    return values


def gray_kernel(chunks, weights_ref, field_ref, out_ref):
    cam = pl.program_id(0)
    rows = pl.ds(pl.multiple_of(cam * 16, 16), 16)
    for chunk in range(chunks):
        lanes = slice(chunk * LANES, (chunk + 1) * LANES)
        total = field_ref[0, 0, 0, :, lanes].astype(F32) * weights_ref[0]
        for channel in range(1, 4):
            total = total + field_ref[channel, 0, 0, :, lanes].astype(F32) * weights_ref[channel]
        out_ref[chunk, rows, :] = total.astype(BF16)

    @pl.when(cam == pl.num_programs(0) - 1)
    def _():
        row, lane = iota((16, LANES), 0), iota((16, LANES), 1)
        wanted = jnp.where(row < 3, row + 125, jnp.where(row == 3, 0, jnp.where(row == 4, 127, row - 5)))
        select = jnp.where((row < 8) & (lane == wanted), F32(1.0), F32(0.0)).astype(BF16)
        edges = [
            lax.dot_general(select, out_ref[chunk, 0:128, :], NT, preferred_element_type=F32)
            for chunk in range(chunks)
        ]
        zero = jnp.zeros((16, LANES), F32)
        for chunk in range(chunks):
            left = edges[chunk - 1] if chunk else zero
            right = edges[chunk + 1] if chunk < chunks - 1 else zero
            halo = jnp.where(row < 3, left, jnp.where(row < 5, edges[chunk], right))
            out_ref[chunk, 128:144, :] = halo.astype(BF16)


def turn_kernel(in_ref, out_ref, scratch):
    for i in range(2):
        block = in_ref[0, :, i * 64 : (i + 1) * 64, :].reshape(256, LANES)
        scratch[...] = block.astype(F32)
        for r in range(16):
            out_ref[r, i] = scratch[pl.ds(r, 16, stride=16), :].astype(BF16)


def tensor_of_cameras(field, grad_img):
    slabs = field.reshape(16, 16, LANES)
    zero = jnp.zeros((1, 16, LANES), F32)
    grad_cam = jnp.concatenate([slabs[1:], zero]) - jnp.concatenate([zero, slabs[:-1]])
    grad_img = grad_img.reshape(16, 16, LANES)
    pad = jnp.zeros((2, 16, LANES), F32)
    result = []
    for product in (grad_cam * grad_cam, grad_cam * grad_img, grad_img * grad_img):
        summed = cascade(jnp.concatenate([pad, product, pad]))
        result.append(summed.reshape(256, LANES).astype(BF16))
    return result


def horizontal_kernel(place_ref, in_ref, halo_ref, out_ref, edge, edge_sums):
    c = pl.program_id(0)
    k, u = iota((LANES, LANES), 0), iota((LANES, LANES), 1)
    d = k - u

    @pl.when(c == 0)
    def _():
        eye = ones_where((d == 0, 1.0)).astype(BF16)
        for col in range(4):
            rows = halo_ref[:, col].reshape(128, LANES)
            turned = lax.dot_general(eye, rows, NT, preferred_element_type=F32).astype(BF16)
            for i in range(2):
                edge[i, col * 64 : (col + 1) * 64, :] = turned[i * 64 : (i + 1) * 64]
        same = (k >> 4) == (u >> 4)
        slot = u & 15
        used = same & ((slot == 1) | (slot == 2) | (slot == 5) | (slot == 6))
        grad = ones_where((used & (d == 1), 1.0), (used & (d == -1), -1.0)).astype(BF16)
        for i in range(2):
            values = edge[i]
            grad_img = jnp.dot(values, grad, preferred_element_type=F32)
            for f, part in enumerate(tensor_of_cameras(values.astype(F32), grad_img)):
                edge_sums[f, i] = part

    place, last = place_ref[0], place_ref[1] - 1
    h = k - c * 16
    grad_matrix = jnp.concatenate(
        [
            ones_where((d == 1, 1.0), (d == -1, -1.0)),
            ones_where(((h == 2) & (u == 0), -1.0), ((h == 5) & (u == 127), 1.0)),
        ]
    ).astype(BF16)
    dist = jnp.abs(d)
    unit = 1.0 / 1024.0
    has_left = jnp.where(place > 0, F32(unit), F32(0.0))
    has_right = jnp.where(place < last, F32(unit), F32(0.0))
    left = ones_where(
        ((h == 1) & (u == 0), 1.0), ((h == 2) & (u == 0), 4.0), ((h == 2) & (u == 1), 1.0)
    )
    right = ones_where(
        ((h == 5) & (u == 127), 4.0), ((h == 5) & (u == 126), 1.0), ((h == 6) & (u == 127), 1.0)
    )
    smooth_matrix = jnp.concatenate(
        [
            ones_where((dist == 0, 6.0 * unit), (dist == 1, 4.0 * unit), (dist == 2, unit)),
            left * has_left + right * has_right,
        ]
    ).astype(BF16)
    for i in range(2):
        values = in_ref[0, :, i * 64 : (i + 1) * 64, :].reshape(256, LANES)
        grad_img = jnp.dot(
            jnp.concatenate([values, edge[i]], axis=1), grad_matrix, preferred_element_type=F32
        )
        for f, part in enumerate(tensor_of_cameras(values.astype(F32), grad_img)):
            out_ref[f, i] = jnp.dot(
                jnp.concatenate([part, edge_sums[f, i]], axis=1),
                smooth_matrix,
                preferred_element_type=F32,
            )


def parts_of(jaa, jab, jbb):
    spread, total = jaa - jbb, jaa + jbb
    twice = jab + jab
    return spread * spread + twice * twice, total * total + 0.1, -jab, jbb + 0.1


def merge(horizontal, vertical):
    nh, dh, bh, ah = parts_of(*horizontal)
    nv, dv, bv, av = parts_of(*vertical)
    p, q = nh * dv, nv * dh
    top = p * (bh * av) + q * (bv * ah)
    return top / ((p + q + 0.1 * (dh * dv)) * (ah * av))


def vertical_kernel(place_ref, gray_ref, low_ref, high_ref, hor_ref, out_ref, field, sums, turned):
    s = pl.program_id(0)

    @pl.when(s == 0)
    def _():
        scale = F32(1.0 / 32.0)

        def load(r, _):
            field[r + 3] = gray_ref[r].astype(F32) * scale
            return 0

        lax.fori_loop(0, 16, load, 0)
        for r in range(3):
            field[r] = low_ref[r].astype(F32) * scale
            field[r + 19] = high_ref[r].astype(F32) * scale

        def row(r, _):
            for half in range(2):
                t = slice(half * 8, half * 8 + 8)
                here = field[r + 1, :, t, :]
                zero = jnp.zeros((1, 8, LANES), F32)
                grad_cam = jnp.concatenate([here[1:], zero]) - jnp.concatenate([zero, here[:-1]])
                grad_img = field[r + 2, :, t, :] - field[r, :, t, :]
                pad = jnp.zeros((2, 8, LANES), F32)
                for f, product in enumerate(
                    (grad_cam * grad_cam, grad_cam * grad_img, grad_img * grad_img)
                ):
                    sums[f, r, :, t, :] = cascade(jnp.concatenate([pad, product, pad]))
            return 0

        lax.fori_loop(0, 20, row, 0)

        @pl.when(place_ref[0] == 0)
        def _():
            for f in range(3):
                sums[f, 0:2] = jnp.zeros((2, 16, 16, LANES), F32)

        @pl.when(place_ref[0] == place_ref[1] - 1)
        def _():
            for f in range(3):
                sums[f, 18:20] = jnp.zeros((2, 16, 16, LANES), F32)

    for block in range(4):
        vertical = [cascade(sums[f, block * 4 : block * 4 + 8, s]) for f in range(3)]
        for step in range(4):
            r = block * 4 + step
            horizontal = [hor_ref[f, 0, pl.ds(r, 16, stride=16), :] for f in range(3)]
            turned[pl.ds(r, 16, stride=16), :] = merge(horizontal, [v[step] for v in vertical])
    out_ref[0, :, 0] = turned[...].astype(BF16).reshape(4, 64, LANES)


def spread_kernel(chunks, in_ref, out_ref):
    for chunk in range(chunks):
        out_ref[:, chunk * LANES : (chunk + 1) * LANES] = in_ref[chunk].astype(F32)


def per_device(light_field, channel_weights):
    group = ("crow", "ccol")
    chunks = lax.axis_size(group)
    band, bands = lax.axis_index("band"), lax.axis_size("band")
    params = functools.partial(pltpu.CompilerParams, vmem_limit_bytes=48 * MIB)
    smem = pl.BlockSpec(memory_space=pltpu.SMEM)

    packed = pl.pallas_call(
        functools.partial(gray_kernel, chunks),
        grid=(8,),
        in_specs=[
            smem,
            pl.BlockSpec((4, 1, 1, 16, 4096), lambda n: (0, n // 4, n % 4, 0, 0)),
        ],
        out_specs=pl.BlockSpec((chunks, 144, LANES), lambda n: (0, 0, 0)),
        out_shape=jax.ShapeDtypeStruct((chunks, 144, LANES), BF16),
        compiler_params=params(),
        name="gray",
    )(channel_weights, light_field)
    columns = lax.all_to_all(packed, group, 0, 0, tiled=True).reshape(8, 4, 144, LANES)

    turned = pl.pallas_call(
        turn_kernel,
        grid=(8,),
        in_specs=[pl.BlockSpec((1, 4, 144, LANES), lambda c: (c, 0, 0, 0))],
        out_specs=pl.BlockSpec((16, 2, 16, LANES), lambda c: (0, c, 0, 0)),
        out_shape=jax.ShapeDtypeStruct((16, 16, 16, LANES), BF16),
        scratch_shapes=[pltpu.VMEM((256, LANES), F32)],
        compiler_params=params(),
        name="turn",
    )(columns)
    low = lax.ppermute(turned[13:16], "band", [(n, n + 1) for n in range(bands - 1)])
    high = lax.ppermute(turned[0:3], "band", [(n + 1, n) for n in range(bands - 1)])

    hor = pl.pallas_call(
        horizontal_kernel,
        grid=(8,),
        in_specs=[
            smem,
            pl.BlockSpec((1, 4, 144, LANES), lambda c: (c, 0, 0, 0)),
            pl.BlockSpec((8, 4, 16, LANES), lambda c: (0, 0, 8, 0)),
        ],
        out_specs=pl.BlockSpec((3, 2, 256, LANES), lambda c: (0, c, 0, 0)),
        out_shape=jax.ShapeDtypeStruct((3, 16, 256, LANES), F32),
        scratch_shapes=[
            pltpu.VMEM((2, 256, LANES), BF16),
            pltpu.VMEM((3, 2, 256, LANES), BF16),
        ],
        compiler_params=params(),
        cost_estimate=pl.CostEstimate(flops=10**9, bytes_accessed=8 * MIB, transcendentals=0),
        name="horizontal",
    )(jnp.stack([lax.axis_index(group), chunks]).astype(jnp.int32), columns, columns)

    depth = pl.pallas_call(
        vertical_kernel,
        grid=(16,),
        in_specs=[
            smem,
            pl.BlockSpec((16, 16, 16, LANES), lambda s: (0, 0, 0, 0)),
            pl.BlockSpec((3, 16, 16, LANES), lambda s: (0, 0, 0, 0)),
            pl.BlockSpec((3, 16, 16, LANES), lambda s: (0, 0, 0, 0)),
            pl.BlockSpec((3, 1, 256, LANES), lambda s: (0, s, 0, 0)),
        ],
        out_specs=pl.BlockSpec((1, 4, 1, 64, LANES), lambda s: (s // 2, 0, s % 2, 0, 0)),
        out_shape=jax.ShapeDtypeStruct((8, 4, 2, 64, LANES), BF16),
        scratch_shapes=[
            pltpu.VMEM((22, 16, 16, LANES), F32),
            pltpu.VMEM((3, 20, 16, 16, LANES), F32),
            pltpu.VMEM((256, LANES), F32),
        ],
        compiler_params=params(),
        name="vertical",
    )(jnp.stack([band, bands]).astype(jnp.int32), turned, low, high, hor)

    back = lax.all_to_all(depth.reshape(chunks, 128, LANES), group, 0, 0, tiled=True)
    out = pl.pallas_call(
        functools.partial(spread_kernel, chunks),
        grid=(4,),
        in_specs=[pl.BlockSpec((chunks, 32, LANES), lambda n: (0, n, 0))],
        out_specs=pl.BlockSpec((32, chunks * LANES), lambda n: (n, 0)),
        out_shape=jax.ShapeDtypeStruct((128, chunks * LANES), F32),
        compiler_params=params(),
        name="spread",
    )(back)
    return out.reshape(2, 4, 16, chunks * LANES)


def solution(mesh):
    placed = (P(None, "crow", "ccol", "band", None), P())
    return jax.shard_map(
        per_device,
        mesh=mesh,
        in_specs=placed,
        out_specs=P("crow", "ccol", "band", None),
        check_vma=False,
    )
```

```python
import functools

import jax
import jax.numpy as jnp
from jax import lax
from jax.experimental import pallas as pl
from jax.experimental.pallas import tpu as pltpu
from jax.sharding import PartitionSpec as P

F32, BF16 = jnp.float32, jnp.bfloat16
LANES = 128
MIB = 1 << 20
NT = (((1,), (1,)), ((), ()))


def iota(shape, dim):
    return lax.broadcasted_iota(jnp.int32, shape, dim)


def ones_where(*conditions_and_values):
    total = None
    for condition, value in conditions_and_values:
        term = jnp.where(condition, F32(value), F32(0.0))
        total = term if total is None else total + term
    return total


def gray_kernel(chunks, weights_ref, field_ref, out_ref, field, arrived):
    copies = [
        pltpu.make_async_copy(field_ref.at[:, cam // 4, cam % 4], field.at[cam], arrived.at[cam])
        for cam in range(8)
    ]
    for copy in copies:
        copy.start()
    for cam in range(8):
        copies[cam].wait()
        for chunk in range(chunks):
            lanes = slice(chunk * LANES, (chunk + 1) * LANES)
            total = field[cam, 0, :, lanes].astype(F32) * weights_ref[0]
            for channel in range(1, 4):
                total = total + field[cam, channel, :, lanes].astype(F32) * weights_ref[channel]
            out_ref[chunk, cam * 16 : (cam + 1) * 16, :] = total.astype(BF16)
    row, lane = iota((16, LANES), 0), iota((16, LANES), 1)
    wanted = jnp.where(row < 3, row + 125, jnp.where(row == 3, 0, jnp.where(row == 4, 127, row - 5)))
    select = jnp.where((row < 8) & (lane == wanted), F32(1.0), F32(0.0)).astype(BF16)
    edges = [
        lax.dot_general(select, out_ref[chunk, 0:128, :], NT, preferred_element_type=F32)
        for chunk in range(chunks)
    ]
    zero = jnp.zeros((16, LANES), F32)
    for chunk in range(chunks):
        left = edges[chunk - 1] if chunk else zero
        right = edges[chunk + 1] if chunk < chunks - 1 else zero
        halo = jnp.where(row < 3, left, jnp.where(row < 5, edges[chunk], right))
        out_ref[chunk, 128:144, :] = halo.astype(BF16)


def turn_kernel(in_ref, out_ref, scratch):
    for c in range(8):
        for i in range(2):
            s = c * 2 + i
            block = in_ref[c, :, i * 64 : (i + 1) * 64, :].reshape(256, LANES)
            scratch[s] = block.astype(F32)
            for r in range(16):
                out_ref[r, s] = scratch[s, pl.ds(r, 16, stride=16), :].astype(BF16)


class Smoother:
    def __init__(self):
        self.last = [None] * 4

    def push(self, value):
        for n in range(4):
            before, self.last[n] = self.last[n], value
            if before is not None:
                value = before if value is None else value + before
        return value


def tensor_of_cameras(field, grad_img):
    count = len(field)
    smoothers = [Smoother() for _ in range(3)]
    result = [[] for _ in range(3)]
    for t in range(count + 2):
        products = (None,) * 3
        if t < count:
            if t == 0:
                grad_cam = -field[1]
            elif t == count - 1:
                grad_cam = field[t - 1]
            else:
                grad_cam = field[t - 1] - field[t + 1]
            products = (grad_cam * grad_cam, grad_cam * grad_img[t], grad_img[t] * grad_img[t])
        for f in range(3):
            value = smoothers[f].push(products[f])
            if t >= 2:
                result[f].append(value.astype(BF16))
    return result


def split(values):
    return [values[n * 16 : (n + 1) * 16] for n in range(values.shape[0] // 16)]


def horizontal_kernel(place_ref, in_ref, out_ref, edge, edge_sums, grads, smooths):
    k, u = iota((LANES, LANES), 0), iota((LANES, LANES), 1)
    d = k - u
    dist = jnp.abs(d)
    eye = ones_where((d == 0, 1.0)).astype(BF16)
    for col in range(4):
        rows = in_ref[:, col, 128:144, :].reshape(128, LANES)
        moved = lax.dot_general(eye, rows, NT, preferred_element_type=F32).astype(BF16)
        for i in range(2):
            edge[i, col * 64 : (col + 1) * 64, :] = moved[i * 64 : (i + 1) * 64]
    slot = u & 15
    used = ((k >> 4) == (u >> 4)) & ((slot == 1) | (slot == 2) | (slot == 5) | (slot == 6))
    grad = ones_where((used & (d == 1), 1.0), (used & (d == -1), -1.0)).astype(BF16)
    for i in range(2):
        values = edge[i]
        grad_img = jnp.dot(values, grad, preferred_element_type=F32)
        summed = tensor_of_cameras(split(values.astype(F32)), split(grad_img))
        for f in range(3):
            for t in range(16):
                edge_sums[f, i, t * 16 : (t + 1) * 16, :] = summed[f][t]

    place, last = place_ref[0], place_ref[1] - 1
    unit = 1.0 / 1024.0
    has_left = jnp.where(place > 0, F32(unit), F32(0.0))
    has_right = jnp.where(place < last, F32(unit), F32(0.0))
    h, col = iota((16, LANES), 0), iota((16, LANES), 1)
    grad_edge = ones_where(((h == 2) & (col == 0), -1.0), ((h == 5) & (col == 127), 1.0))
    left = ones_where(
        ((h == 1) & (col == 0), 1.0), ((h == 2) & (col == 0), 4.0), ((h == 2) & (col == 1), 1.0)
    )
    right = ones_where(
        ((h == 5) & (col == 127), 4.0),
        ((h == 5) & (col == 126), 1.0),
        ((h == 6) & (col == 127), 1.0),
    )
    smooth_edge = (left * has_left + right * has_right).astype(BF16)
    grad_edge = grad_edge.astype(BF16)
    grad_own = ones_where((d == 1, 1.0), (d == -1, -1.0)).astype(BF16)
    smooth_own = ones_where(
        (dist == 0, 6.0 * unit), (dist == 1, 4.0 * unit), (dist == 2, unit)
    ).astype(BF16)
    zero = jnp.zeros((16, LANES), BF16)
    for c in range(8):
        for matrix, own, side in ((grads, grad_own, grad_edge), (smooths, smooth_own, smooth_edge)):
            matrix[c, 0:128, :] = own
            for n in range(8):
                matrix[c, 128 + n * 16 : 144 + n * 16, :] = side if n == c else zero

    @pl.loop(0, 8)
    def _(c):
        for i in range(2):
            values = in_ref[c, :, i * 64 : (i + 1) * 64, :].reshape(256, LANES)
            grad_img = jnp.dot(
                jnp.concatenate([values, edge[i]], axis=1), grads[c], preferred_element_type=F32
            )
            summed = tensor_of_cameras(split(values.astype(F32)), split(grad_img))
            for f in range(3):
                part = jnp.concatenate(summed[f])
                out_ref[f, c * 2 + i] = jnp.dot(
                    jnp.concatenate([part, edge_sums[f, i]], axis=1),
                    smooths[c],
                    preferred_element_type=F32,
                )


def parts_of(jaa, jab, jbb):
    spread, total = jaa - jbb, jaa + jbb
    twice = jab + jab
    return spread * spread + twice * twice, total * total + 0.1, jab, jbb + 0.1


def merge(horizontal, vertical):
    nh, dh, bh, ah = parts_of(*horizontal)
    nv, dv, bv, av = parts_of(*vertical)
    p, q = nh * dv, nv * dh
    top = p * (bh * av) + q * (bv * ah)
    return top / ((p + q + 0.1 * (dh * dv)) * (ah * av))


def vertical_kernel(place_ref, gray_ref, low_ref, high_ref, hor_ref, out_ref, field, sums, turned):
    scale = F32(1.0 / 32.0)
    zero = jnp.zeros((22, 16, LANES), F32)
    field[0] = zero
    field[17] = zero

    @pl.loop(0, 16)
    def _(r):
        for s in range(16):
            field[s + 1, r + 3] = gray_ref[r, s].astype(F32) * scale

    for r in range(3):
        for s in range(16):
            field[s + 1, r] = low_ref[r, s].astype(F32) * scale
            field[s + 1, r + 19] = high_ref[r, s].astype(F32) * scale

    has_low = jnp.where(place_ref[0] > 0, F32(1.0), F32(0.0))
    has_high = jnp.where(place_ref[0] < place_ref[1] - 1, F32(1.0), F32(0.0))

    @pl.loop(0, 16)
    def _(s):
        smoothers = [Smoother() for _ in range(3)]
        for q in range(20):
            grad_cam = field[s, q + 1] - field[s + 2, q + 1]
            grad_img = field[s + 1, q + 2] - field[s + 1, q]
            if q < 2:
                grad_img = grad_img * has_low
            if q >= 18:
                grad_img = grad_img * has_high
            products = (grad_cam * grad_cam, grad_cam * grad_img, grad_img * grad_img)
            for f in range(3):
                value = smoothers[f].push(products[f])
                if q >= 4:
                    sums[f, s, q - 4] = value

    @pl.loop(0, 16)
    def _(r):
        smoothers = [Smoother() for _ in range(3)]
        rows = pl.ds(r, 16, stride=16)
        for s in range(18):
            vertical = [
                smoothers[f].push(sums[f, s, r] if s < 16 else None) for f in range(3)
            ]
            if s >= 2:
                horizontal = [hor_ref[f, s - 2, rows, :] for f in range(3)]
                turned[s - 2, rows, :] = merge(horizontal, vertical)

    @pl.loop(0, 8)
    def _(c):
        for i in range(2):
            out_ref[c, :, i] = turned[c * 2 + i].astype(BF16).reshape(4, 64, LANES)


def spread_kernel(chunks, in_ref, out_ref, scratch, sent):
    copies = []
    for part in range(8):
        rows = slice(part * 16, (part + 1) * 16)
        for chunk in range(chunks):
            scratch[rows, chunk * LANES : (chunk + 1) * LANES] = in_ref[chunk, rows, :].astype(F32)
        copy = pltpu.make_async_copy(scratch.at[rows], out_ref.at[rows], sent.at[part])
        copy.start()
        copies.append(copy)
    for copy in copies:
        copy.wait()


def per_device(light_field, channel_weights):
    group = ("crow", "ccol")
    chunks = lax.axis_size(group)
    band, bands = lax.axis_index("band"), lax.axis_size("band")
    params = lambda mib: pltpu.CompilerParams(vmem_limit_bytes=mib * MIB)
    smem = pl.BlockSpec(memory_space=pltpu.SMEM)
    vmem = pl.BlockSpec(memory_space=pltpu.VMEM)
    hbm = pl.BlockSpec(memory_space=pl.ANY)

    packed = pl.pallas_call(
        functools.partial(gray_kernel, chunks),
        in_specs=[smem, hbm],
        out_specs=vmem,
        out_shape=jax.ShapeDtypeStruct((chunks, 144, LANES), BF16),
        scratch_shapes=[pltpu.VMEM((8, 4, 16, chunks * LANES), BF16), pltpu.SemaphoreType.DMA((8,))],
        compiler_params=params(58),
        name="gray",
    )(channel_weights, light_field)
    columns = lax.all_to_all(packed, group, 0, 0, tiled=True).reshape(8, 4, 144, LANES)

    turned = pl.pallas_call(
        turn_kernel,
        in_specs=[vmem],
        out_specs=vmem,
        out_shape=jax.ShapeDtypeStruct((16, 16, 16, LANES), BF16),
        scratch_shapes=[pltpu.VMEM((16, 256, LANES), F32)],
        compiler_params=params(16),
        name="turn",
    )(columns)
    low = lax.ppermute(turned[13:16], "band", [(n, n + 1) for n in range(bands - 1)])
    high = lax.ppermute(turned[0:3], "band", [(n + 1, n) for n in range(bands - 1)])

    hor = pl.pallas_call(
        horizontal_kernel,
        in_specs=[smem, vmem],
        out_specs=vmem,
        out_shape=jax.ShapeDtypeStruct((3, 16, 256, LANES), F32),
        scratch_shapes=[
            pltpu.VMEM((2, 256, LANES), BF16),
            pltpu.VMEM((3, 2, 256, LANES), BF16),
            pltpu.VMEM((8, 256, LANES), BF16),
            pltpu.VMEM((8, 256, LANES), BF16),
        ],
        compiler_params=params(24),
        cost_estimate=pl.CostEstimate(flops=10**9, bytes_accessed=8 * MIB, transcendentals=0),
        name="horizontal",
    )(jnp.stack([lax.axis_index(group), chunks]).astype(jnp.int32), columns)

    depth = pl.pallas_call(
        vertical_kernel,
        in_specs=[smem, vmem, vmem, vmem, vmem],
        out_specs=vmem,
        out_shape=jax.ShapeDtypeStruct((8, 4, 2, 64, LANES), BF16),
        scratch_shapes=[
            pltpu.VMEM((18, 22, 16, LANES), F32),
            pltpu.VMEM((3, 16, 16, 16, LANES), F32),
            pltpu.VMEM((16, 256, LANES), F32),
        ],
        compiler_params=params(32),
        name="vertical",
    )(jnp.stack([band, bands]).astype(jnp.int32), turned, low, high, hor)

    back = lax.all_to_all(depth.reshape(chunks, 128, LANES), group, 0, 0, tiled=True)
    out = pl.pallas_call(
        functools.partial(spread_kernel, chunks),
        in_specs=[vmem],
        out_specs=hbm,
        out_shape=jax.ShapeDtypeStruct((128, chunks * LANES), F32),
        scratch_shapes=[pltpu.VMEM((128, chunks * LANES), F32), pltpu.SemaphoreType.DMA((8,))],
        compiler_params=params(58),
        name="spread",
    )(back)
    return out.reshape(2, 4, 16, chunks * LANES)


def solution(mesh):
    placed = (P(None, "crow", "ccol", "band", None), P())
    return jax.shard_map(
        per_device,
        mesh=mesh,
        in_specs=placed,
        out_specs=P("crow", "ccol", "band", None),
        check_vma=False,
    )
```

```python
import functools

import jax
import jax.numpy as jnp
from jax import lax
from jax.experimental import pallas as pl
from jax.experimental.pallas import tpu as pltpu
from jax.sharding import PartitionSpec as P

F32, BF16 = jnp.float32, jnp.bfloat16
LANES = 128
MIB = 1 << 20
NT = (((1,), (1,)), ((), ()))


def iota(shape, dim):
    return lax.broadcasted_iota(jnp.int32, shape, dim)


def ones_where(*conditions_and_values):
    total = None
    for condition, value in conditions_and_values:
        term = jnp.where(condition, F32(value), F32(0.0))
        total = term if total is None else total + term
    return total


def gray_kernel(chunks, weights_hbm, field_ref, out_ref, field, edges, weights_ref, arrived, known):
    def incoming(cam):
        return pltpu.make_async_copy(
            field_ref.at[:, cam // 4, cam % 4], field.at[cam], arrived.at[cam]
        )

    weights_copy = pltpu.make_async_copy(weights_hbm, weights_ref, known)
    weights_copy.start()
    for cam in range(8):
        incoming(cam).start()
    row, lane = iota((16, LANES), 0), iota((16, LANES), 1)
    wanted = jnp.where(row < 3, row + 125, jnp.where(row == 3, 0, jnp.where(row == 4, 127, row - 5)))
    select = jnp.where((row < 8) & (lane == wanted), F32(1.0), F32(0.0)).astype(BF16)
    edges[0] = jnp.zeros((16, LANES), F32)
    edges[chunks + 1] = jnp.zeros((16, LANES), F32)
    weights_copy.wait()
    weights = [weights_ref[channel] for channel in range(4)]

    @pl.loop(0, 8)
    def _(cam):
        incoming(cam).wait()
        rows = pl.ds(pl.multiple_of(cam * 16, 16), 16)
        for chunk in range(chunks):
            lanes = slice(chunk * LANES, (chunk + 1) * LANES)
            total = field[cam, 0, :, lanes].astype(F32) * weights[0]
            for channel in range(1, 4):
                total = total + field[cam, channel, :, lanes].astype(F32) * weights[channel]
            out_ref[chunk, rows, :] = total.astype(BF16)

    @pl.loop(0, chunks, unroll=32)
    def _(chunk):
        edges[chunk + 1] = lax.dot_general(
            select, out_ref[chunk, 0:128, :], NT, preferred_element_type=F32
        )

    @pl.loop(0, chunks, unroll=32)
    def _(chunk):
        halo = jnp.where(row < 3, edges[chunk], jnp.where(row < 5, edges[chunk + 1], edges[chunk + 2]))
        out_ref[chunk, 128:144, :] = halo.astype(BF16)


PITCH = 17


def edges_kernel(in_ref, first_ref, last_ref, scratch):
    for c in range(8):
        for i in range(2):
            s = c * 2 + i
            for t in range(16):
                rows = slice(i * 64 + t % 4 * 16, i * 64 + t % 4 * 16 + 16)
                scratch[s, t * PITCH : t * PITCH + 16, :] = in_ref[c, t // 4, rows, :].astype(F32)
            for r in range(3):
                first_ref[r, s] = scratch[s, pl.ds(r, 16, stride=PITCH), :].astype(BF16)
                last_ref[r, s] = scratch[s, pl.ds(r + 13, 16, stride=PITCH), :].astype(BF16)


class Smoother:
    def __init__(self):
        self.last = [None] * 4

    def push(self, value):
        for n in range(4):
            before, self.last[n] = self.last[n], value
            if before is not None:
                value = before if value is None else value + before
        return value


def tensor_of_cameras(field, grad_img):
    count = len(field)
    smoothers = [Smoother() for _ in range(3)]
    result = [[] for _ in range(3)]
    for t in range(count + 2):
        products = (None,) * 3
        if t < count:
            if t == 0:
                grad_cam = -field[1]
            elif t == count - 1:
                grad_cam = field[t - 1]
            else:
                grad_cam = field[t - 1] - field[t + 1]
            products = (grad_cam * grad_cam, grad_cam * grad_img[t], grad_img[t] * grad_img[t])
        for f in range(3):
            value = smoothers[f].push(products[f])
            if t >= 2:
                result[f].append(value.astype(BF16))
    return result


def split(values):
    return [values[n * 16 : (n + 1) * 16] for n in range(values.shape[0] // 16)]


def horizontal_kernel(in_ref, out_ref, gray_ref, edge, edge_sums, grads, smooths, scratch):
    k, u = iota((LANES, LANES), 0), iota((LANES, LANES), 1)
    d = k - u
    dist = jnp.abs(d)
    eye = ones_where((d == 0, 1.0)).astype(BF16)
    for col in range(4):
        rows = in_ref[:, col, 128:144, :].reshape(128, LANES)
        moved = lax.dot_general(eye, rows, NT, preferred_element_type=F32).astype(BF16)
        for i in range(2):
            edge[i, col * 64 : (col + 1) * 64, :] = moved[i * 64 : (i + 1) * 64]
    slot = u & 15
    used = ((k >> 4) == (u >> 4)) & ((slot == 1) | (slot == 2) | (slot == 5) | (slot == 6))
    grad = ones_where((used & (d == 1), 1.0), (used & (d == -1), -1.0)).astype(BF16)
    for i in range(2):
        values = edge[i]
        grad_img = jnp.dot(values, grad, preferred_element_type=F32)
        summed = tensor_of_cameras(split(values.astype(F32)), split(grad_img))
        for f in range(3):
            for t in range(16):
                edge_sums[f, i, t * 16 : (t + 1) * 16, :] = summed[f][t]

    group = ("crow", "ccol")
    place, last = lax.axis_index(group), lax.axis_size(group) - 1
    unit = 1.0 / 1024.0
    has_left = jnp.where(place > 0, F32(unit), F32(0.0))
    has_right = jnp.where(place < last, F32(unit), F32(0.0))
    h, col = iota((16, LANES), 0), iota((16, LANES), 1)
    grad_edge = ones_where(((h == 2) & (col == 0), -1.0), ((h == 5) & (col == 127), 1.0))
    left = ones_where(
        ((h == 1) & (col == 0), 1.0), ((h == 2) & (col == 0), 4.0), ((h == 2) & (col == 1), 1.0)
    )
    right = ones_where(
        ((h == 5) & (col == 127), 4.0),
        ((h == 5) & (col == 126), 1.0),
        ((h == 6) & (col == 127), 1.0),
    )
    smooth_edge = (left * has_left + right * has_right).astype(BF16)
    grad_edge = grad_edge.astype(BF16)
    grad_own = ones_where((d == 1, 1.0), (d == -1, -1.0)).astype(BF16)
    smooth_own = ones_where(
        (dist == 0, 6.0 * unit), (dist == 1, 4.0 * unit), (dist == 2, unit)
    ).astype(BF16)
    zero = jnp.zeros((16, LANES), BF16)
    for c in range(8):
        for matrix, own, side in ((grads, grad_own, grad_edge), (smooths, smooth_own, smooth_edge)):
            matrix[c, 0:128, :] = own
            for n in range(8):
                matrix[c, 128 + n * 16 : 144 + n * 16, :] = side if n == c else zero

    def values_of(c, i):
        return in_ref[c, :, i * 64 : (i + 1) * 64, :].reshape(256, LANES)

    def gradient(c):
        own = jnp.concatenate([values_of(c, 0), values_of(c, 1)])
        side = jnp.concatenate([edge[0], edge[1]])
        return jnp.dot(
            jnp.concatenate([own, side], axis=1), grads[c], preferred_element_type=F32
        )

    def products(c, grad_img):
        summed = []
        for i in range(2):
            field = split(values_of(c, i).astype(F32))
            for t in range(16):
                scratch[c * 2 + i, t * PITCH : t * PITCH + 16, :] = field[t]
            for r in range(16):
                gray_ref[c * 2 + i, r] = scratch[c * 2 + i, pl.ds(r, 16, stride=PITCH), :]
            summed.append(tensor_of_cameras(field, split(grad_img[i * 256 : (i + 1) * 256])))
        return jnp.concatenate([v for f in range(3) for i in range(2) for v in summed[i][f]])

    def smooth(c, parts):
        side = jnp.concatenate([edge_sums[f, i] for f in range(3) for i in range(2)])
        full = jnp.dot(
            jnp.concatenate([parts, side], axis=1), smooths[c], preferred_element_type=F32
        )
        for f in range(3):
            for i in range(2):
                n = (f * 2 + i) * 256
                out_ref[f, c * 2 + i] = full[n : n + 256]

    grad_img, parts = gradient(0), None
    for c in range(8):
        following = gradient(c + 1) if c < 7 else None
        now = products(c, grad_img)
        if c:
            smooth(c - 1, parts)
        grad_img, parts = following, now
    smooth(7, parts)


def parts_of(jaa, jab, jbb, scale):
    spread, total = jaa - jbb, jaa + jbb
    twice = jab + jab
    near = F32(0.1 * scale)
    return spread * spread + twice * twice, total * total + near * F32(scale), jab, jbb + near


def merge(horizontal, vertical):
    nh, dh, bh, ah = parts_of(*horizontal, 1.0)
    nv, dv, bv, av = parts_of(*vertical, 1024.0)
    p, q = nh * dv, nv * dh
    top = p * (bh * av) + q * (bv * ah)
    return top / ((p + q + 0.1 * (dh * dv)) * (ah * av))


def vertical_kernel(gray_ref, low_ref, high_ref, hor_ref, out_ref, sums):
    band, last = lax.axis_index("band"), lax.axis_size("band") - 1
    has_low = jnp.where(band > 0, F32(1.0), F32(0.0))
    has_high = jnp.where(band < last, F32(1.0), F32(0.0))

    def field(s, r):
        if r < 0:
            return low_ref[r + 3, s].astype(F32)
        return gray_ref[s, r] if r < 16 else high_ref[r - 16, s].astype(F32)

    for s in range(16):
        smoothers = [Smoother() for _ in range(3)]
        for q in range(20):
            r = q - 2
            if s == 0:
                grad_cam = -field(1, r)
            elif s == 15:
                grad_cam = field(14, r)
            else:
                grad_cam = field(s - 1, r) - field(s + 1, r)
            grad_img = field(s, r + 1) - field(s, r - 1)
            if r < 0:
                grad_img = grad_img * has_low
            if r >= 16:
                grad_img = grad_img * has_high
            products = (grad_cam * grad_cam, grad_cam * grad_img, grad_img * grad_img)
            for f in range(3):
                value = smoothers[f].push(products[f])
                if q >= 4:
                    sums[f, s, pl.ds(q - 4, 16, stride=PITCH), :] = value

    for t in range(16):
        smoothers = [Smoother() for _ in range(3)]
        for s in range(18):
            vertical = [
                smoothers[f].push(sums[f, s, t * PITCH : t * PITCH + 16, :] if s < 16 else None)
                for f in range(3)
            ]
            if s >= 2:
                c, i = (s - 2) // 2, (s - 2) % 2
                horizontal = [hor_ref[f, s - 2, t * 16 : (t + 1) * 16, :] for f in range(3)]
                rows = slice(t % 4 * 16, t % 4 * 16 + 16)
                out_ref[c, t // 4, i, rows, :] = merge(horizontal, vertical).astype(BF16)


def spread_kernel(chunks, in_ref, out_ref, scratch, sent):
    copies = []
    for part in range(8):
        rows = slice(part * 16, (part + 1) * 16)
        for chunk in range(chunks):
            scratch[rows, chunk * LANES : (chunk + 1) * LANES] = in_ref[chunk, rows, :].astype(F32)
        copy = pltpu.make_async_copy(scratch.at[rows], out_ref.at[rows], sent.at[part])
        copy.start()
        copies.append(copy)
    for copy in copies:
        copy.wait()


def per_device(light_field, channel_weights):
    group = ("crow", "ccol")
    chunks = lax.axis_size(group)
    bands = lax.axis_size("band")
    params = lambda mib: pltpu.CompilerParams(vmem_limit_bytes=mib * MIB)
    vmem = pl.BlockSpec(memory_space=pltpu.VMEM)
    hbm = pl.BlockSpec(memory_space=pl.ANY)

    packed = pl.pallas_call(
        functools.partial(gray_kernel, chunks),
        in_specs=[hbm, hbm],
        out_specs=vmem,
        out_shape=jax.ShapeDtypeStruct((chunks, 144, LANES), BF16),
        scratch_shapes=[
            pltpu.VMEM((8, 4, 16, chunks * LANES), BF16),
            pltpu.VMEM((chunks + 2, 16, LANES), F32),
            pltpu.SMEM((4,), F32),
            pltpu.SemaphoreType.DMA((8,)),
            pltpu.SemaphoreType.DMA,
        ],
        compiler_params=params(58),
        name="gray",
    )(channel_weights, light_field)
    columns = lax.all_to_all(packed, group, 0, 0, tiled=True).reshape(8, 4, 144, LANES)

    first, final = pl.pallas_call(
        edges_kernel,
        in_specs=[vmem],
        out_specs=[vmem, vmem],
        out_shape=[jax.ShapeDtypeStruct((3, 16, 16, LANES), BF16)] * 2,
        scratch_shapes=[pltpu.VMEM((16, 16 * PITCH, LANES), F32)],
        compiler_params=params(16),
        name="edges",
    )(columns)
    low = lax.ppermute(final, "band", [(n, n + 1) for n in range(bands - 1)])
    high = lax.ppermute(first, "band", [(n + 1, n) for n in range(bands - 1)])

    hor, gray = pl.pallas_call(
        horizontal_kernel,
        in_specs=[vmem],
        out_specs=[vmem, vmem],
        out_shape=[
            jax.ShapeDtypeStruct((3, 16, 256, LANES), F32),
            jax.ShapeDtypeStruct((16, 16, 16, LANES), F32),
        ],
        scratch_shapes=[
            pltpu.VMEM((2, 256, LANES), BF16),
            pltpu.VMEM((3, 2, 256, LANES), BF16),
            pltpu.VMEM((8, 256, LANES), BF16),
            pltpu.VMEM((8, 256, LANES), BF16),
            pltpu.VMEM((16, 16 * PITCH, LANES), F32),
        ],
        compiler_params=params(24),
        cost_estimate=pl.CostEstimate(flops=10**9, bytes_accessed=8 * MIB, transcendentals=0),
        name="horizontal",
    )(columns)

    depth = pl.pallas_call(
        vertical_kernel,
        in_specs=[vmem, vmem, vmem, vmem],
        out_specs=vmem,
        out_shape=jax.ShapeDtypeStruct((8, 4, 2, 64, LANES), BF16),
        scratch_shapes=[pltpu.VMEM((3, 16, 16 * PITCH, LANES), F32)],
        compiler_params=params(24),
        name="vertical",
    )(gray, low, high, hor)

    back = lax.all_to_all(depth.reshape(chunks, 128, LANES), group, 0, 0, tiled=True)
    out = pl.pallas_call(
        functools.partial(spread_kernel, chunks),
        in_specs=[vmem],
        out_specs=hbm,
        out_shape=jax.ShapeDtypeStruct((128, chunks * LANES), F32),
        scratch_shapes=[pltpu.VMEM((128, chunks * LANES), F32), pltpu.SemaphoreType.DMA((8,))],
        compiler_params=params(8),
        name="spread",
    )(back)
    return out.reshape(2, 4, 16, chunks * LANES)


def solution(mesh):
    placed = (P(None, "crow", "ccol", "band", None), P())
    return jax.shard_map(
        per_device,
        mesh=mesh,
        in_specs=placed,
        out_specs=P("crow", "ccol", "band", None),
        check_vma=False,
    )
```

```python
import functools

import jax
import jax.numpy as jnp
from jax import lax
from jax.experimental import pallas as pl
from jax.experimental.pallas import tpu as pltpu
from jax.sharding import PartitionSpec as P

F32, BF16 = jnp.float32, jnp.bfloat16
LANES = 128
MIB = 1 << 20
NT = (((1,), (1,)), ((), ()))


def iota(shape, dim):
    return lax.broadcasted_iota(jnp.int32, shape, dim)


def ones_where(*conditions_and_values):
    total = None
    for condition, value in conditions_and_values:
        term = jnp.where(condition, F32(value), F32(0.0))
        total = term if total is None else total + term
    return total


def gray_kernel(chunks, weights_hbm, field_ref, out_ref, field, edges, weights_ref, arrived, known):
    def incoming(cam):
        return pltpu.make_async_copy(
            field_ref.at[:, cam // 4, cam % 4], field.at[cam], arrived.at[cam]
        )

    weights_copy = pltpu.make_async_copy(weights_hbm, weights_ref, known)
    weights_copy.start()
    for cam in range(8):
        incoming(cam).start()
    row, lane = iota((16, LANES), 0), iota((16, LANES), 1)
    wanted = jnp.where(row < 3, row + 125, jnp.where(row == 3, 0, jnp.where(row == 4, 127, row - 5)))
    select = jnp.where((row < 8) & (lane == wanted), F32(1.0), F32(0.0)).astype(BF16)
    edges[0] = jnp.zeros((16, LANES), F32)
    edges[chunks + 1] = jnp.zeros((16, LANES), F32)
    weights_copy.wait()
    weights = [weights_ref[channel] for channel in range(4)]

    @pl.loop(0, 8)
    def _(cam):
        incoming(cam).wait()
        rows = pl.ds(pl.multiple_of(cam * 16, 16), 16)
        for chunk in range(chunks):
            lanes = slice(chunk * LANES, (chunk + 1) * LANES)
            total = field[cam, 0, :, lanes].astype(F32) * weights[0]
            for channel in range(1, 4):
                total = total + field[cam, channel, :, lanes].astype(F32) * weights[channel]
            out_ref[chunk, rows, :] = total.astype(BF16)

    @pl.loop(0, chunks, unroll=32)
    def _(chunk):
        edges[chunk + 1] = lax.dot_general(
            select, out_ref[chunk, 0:128, :], NT, preferred_element_type=F32
        )

    @pl.loop(0, chunks, unroll=32)
    def _(chunk):
        halo = jnp.where(row < 3, edges[chunk], jnp.where(row < 5, edges[chunk + 1], edges[chunk + 2]))
        out_ref[chunk, 128:136, :] = halo[0:8].astype(BF16)


PITCH = 17


def edges_kernel(in_ref, first_ref, last_ref, scratch):
    for c in range(8):
        for i in range(2):
            s = c * 2 + i
            for t in range(16):
                rows = slice(i * 64 + t % 4 * 16, i * 64 + t % 4 * 16 + 16)
                scratch[s, t * PITCH : t * PITCH + 16, :] = in_ref[c, t // 4, rows, :].astype(F32)
            for r in range(3):
                first_ref[r, s] = scratch[s, pl.ds(r, 16, stride=PITCH), :].astype(BF16)
                last_ref[r, s] = scratch[s, pl.ds(r + 13, 16, stride=PITCH), :].astype(BF16)


class Smoother:
    def __init__(self):
        self.last = [None] * 4

    def push(self, value):
        for n in range(4):
            before, self.last[n] = self.last[n], value
            if before is not None:
                value = before if value is None else value + before
        return value


def tensor_of_cameras(field, grad_img):
    count = len(field)
    smoothers = [Smoother() for _ in range(3)]
    result = [[] for _ in range(3)]
    for t in range(count + 2):
        products = (None,) * 3
        if t < count:
            if t == 0:
                grad_cam = -field[1]
            elif t == count - 1:
                grad_cam = field[t - 1]
            else:
                grad_cam = field[t - 1] - field[t + 1]
            products = (grad_cam * grad_cam, grad_cam * grad_img[t], grad_img[t] * grad_img[t])
        for f in range(3):
            value = smoothers[f].push(products[f])
            if t >= 2:
                result[f].append(value.astype(BF16))
    return result


def split(values):
    return [values[n * 16 : (n + 1) * 16] for n in range(values.shape[0] // 16)]


def products_of(field, s, r, factor=None):
    if s == 0:
        grad_cam = -field(1, r)
    elif s == 15:
        grad_cam = field(14, r)
    else:
        grad_cam = field(s - 1, r) - field(s + 1, r)
    grad_img = field(s, r + 1) - field(s, r - 1)
    if factor is not None:
        grad_img = grad_img * factor
    return grad_cam * grad_cam, grad_cam * grad_img, grad_img * grad_img


def merge_rows(rows, sums, hor_ref, depth_ref):
    for n, r in enumerate(rows):
        smoothers = [Smoother() for _ in range(3)]
        lines = pl.ds(r, 16, stride=PITCH)
        for s in range(18):
            vertical = [smoothers[f].push(sums[f, s, n] if s < 16 else None) for f in range(3)]
            if s >= 2:
                horizontal = [hor_ref[f, s - 2, lines, :] for f in range(3)]
                depth_ref[s - 2, lines, :] = merge(horizontal, vertical)


def inner_kernel(
    in_ref, out_ref, gray_ref, depth_ref, edge, edge_sums, grads, smooths, scratch, sums
):
    k, u = iota((LANES, LANES), 0), iota((LANES, LANES), 1)
    d = k - u
    dist = jnp.abs(d)
    eye = ones_where((d == 0, 1.0)).astype(BF16)
    for col in range(4):
        rows = [in_ref[c, col, 128:136, :].astype(F32) for c in range(8)]
        rows = jnp.concatenate(rows + [jnp.zeros((64, LANES), F32)]).astype(BF16)
        moved = lax.dot_general(eye, rows, NT, preferred_element_type=F32).astype(BF16)
        for i in range(2):
            edge[i, col * 64 : (col + 1) * 64, :] = moved[i * 64 : (i + 1) * 64]
    slot = u & 7
    used = ((k >> 3) == (u >> 3)) & ((slot == 1) | (slot == 2) | (slot == 5) | (slot == 6))
    grad = ones_where((used & (d == 1), 1.0), (used & (d == -1), -1.0)).astype(BF16)
    for i in range(2):
        values = edge[i]
        grad_img = jnp.dot(values, grad, preferred_element_type=F32)
        summed = tensor_of_cameras(split(values.astype(F32)), split(grad_img))
        for f in range(3):
            for t in range(16):
                edge_sums[f, i, t * 16 : (t + 1) * 16, :] = summed[f][t]

    group = ("crow", "ccol")
    place, last = lax.axis_index(group), lax.axis_size(group) - 1
    unit = 1.0 / 1024.0
    has_left = jnp.where(place > 0, F32(unit), F32(0.0))
    has_right = jnp.where(place < last, F32(unit), F32(0.0))
    h, col = iota((8, LANES), 0), iota((8, LANES), 1)
    grad_edge = ones_where(((h == 2) & (col == 0), -1.0), ((h == 5) & (col == 127), 1.0))
    left = ones_where(
        ((h == 1) & (col == 0), 1.0), ((h == 2) & (col == 0), 4.0), ((h == 2) & (col == 1), 1.0)
    )
    right = ones_where(
        ((h == 5) & (col == 127), 4.0),
        ((h == 5) & (col == 126), 1.0),
        ((h == 6) & (col == 127), 1.0),
    )
    smooth_edge = left * has_left + right * has_right
    grad_own = ones_where((d == 1, 1.0), (d == -1, -1.0)).astype(BF16)
    smooth_own = ones_where(
        (dist == 0, 6.0 * unit), (dist == 1, 4.0 * unit), (dist == 2, unit)
    ).astype(BF16)
    zero = jnp.zeros((8, LANES), F32)
    for c in range(8):
        for matrix, own, side in ((grads, grad_own, grad_edge), (smooths, smooth_own, smooth_edge)):
            matrix[c, 0:128, :] = own
            for n in range(8):
                pair = [side if n * 2 + m == c else zero for m in range(2)]
                matrix[c, 128 + n * 16 : 144 + n * 16, :] = jnp.concatenate(pair).astype(BF16)

    def values_of(c, i):
        return in_ref[c, :, i * 64 : (i + 1) * 64, :].reshape(256, LANES)

    def gradient(c):
        own = jnp.concatenate([values_of(c, 0), values_of(c, 1)])
        side = jnp.concatenate([edge[0], edge[1]])
        return jnp.dot(
            jnp.concatenate([own, side], axis=1), grads[c], preferred_element_type=F32
        )

    def products(c, grad_img):
        summed = []
        for i in range(2):
            field = split(values_of(c, i).astype(F32))
            for t in range(16):
                scratch[c * 2 + i, t * PITCH : t * PITCH + 16, :] = field[t]
            for r in range(16):
                gray_ref[c * 2 + i, r] = scratch[c * 2 + i, pl.ds(r, 16, stride=PITCH), :]
            summed.append(tensor_of_cameras(field, split(grad_img[i * 256 : (i + 1) * 256])))
        return jnp.concatenate([v for f in range(3) for i in range(2) for v in summed[i][f]])

    def smooth(c, parts):
        side = jnp.concatenate([edge_sums[f, i] for f in range(3) for i in range(2)])
        full = jnp.dot(
            jnp.concatenate([parts, side], axis=1), smooths[c], preferred_element_type=F32
        )
        for f in range(3):
            for i in range(2):
                n = (f * 2 + i) * 256
                for t in range(16):
                    rows = slice(t * PITCH, t * PITCH + 16)
                    out_ref[f, c * 2 + i, rows, :] = full[n + t * 16 : n + t * 16 + 16]

    grad_img, parts = gradient(0), None
    for c in range(8):
        following = gradient(c + 1) if c < 7 else None
        now = products(c, grad_img)
        if c:
            smooth(c - 1, parts)
        grad_img, parts = following, now
    smooth(7, parts)

    for s in range(16):
        smoothers = [Smoother() for _ in range(3)]
        for r in range(1, 15):
            products = products_of(lambda s, r: gray_ref[s, r], s, r)
            for f in range(3):
                value = smoothers[f].push(products[f])
                if r >= 5:
                    sums[f, s, r - 5] = value
    merge_rows(range(3, 13), sums, out_ref, depth_ref)


def parts_of(jaa, jab, jbb, scale):
    spread, total = jaa - jbb, jaa + jbb
    twice = jab + jab
    near = F32(0.1 * scale)
    return spread * spread + twice * twice, total * total + near * F32(scale), jab, jbb + near


def merge(horizontal, vertical):
    nh, dh, bh, ah = parts_of(*horizontal, 1.0)
    nv, dv, bv, av = parts_of(*vertical, 1024.0)
    p, q = nh * dv, nv * dh
    top = p * (bh * av) + q * (bv * ah)
    return top / ((p + q + 0.1 * (dh * dv)) * (ah * av))


def outer_kernel(gray_ref, low_ref, high_ref, hor_ref, inner_ref, out_ref, sums, depth):
    band, last = lax.axis_index("band"), lax.axis_size("band") - 1
    has_low = jnp.where(band > 0, F32(1.0), F32(0.0))
    has_high = jnp.where(band < last, F32(1.0), F32(0.0))

    def field(s, r):
        if r < 0:
            return low_ref[r + 3, s].astype(F32)
        return gray_ref[s, r] if r < 16 else high_ref[r - 16, s].astype(F32)

    for s in range(16):
        for side in range(2):
            smoothers = [Smoother() for _ in range(3)]
            for q in range(7):
                r = q + 11 if side else q - 2
                factor = has_low if r < 0 else has_high if r >= 16 else None
                products = products_of(field, s, r, factor)
                for f in range(3):
                    value = smoothers[f].push(products[f])
                    if q >= 4:
                        sums[f, s, side * 3 + q - 4] = value
    merge_rows((0, 1, 2, 13, 14, 15), sums, hor_ref, depth)

    row = iota((16, LANES), 0)
    is_inner = (row >= 3) & (row < 13)
    for s in range(16):
        for t in range(16):
            lines = slice(t * PITCH, t * PITCH + 16)
            value = jnp.where(is_inner, inner_ref[s, lines, :], depth[s, lines, :])
            rows = slice(t % 4 * 16, t % 4 * 16 + 16)
            out_ref[s // 2, t // 4, s % 2, rows, :] = value.astype(BF16)


def spread_kernel(chunks, in_ref, out_ref, scratch, sent):
    copies = []
    for part in range(8):
        rows = slice(part * 16, (part + 1) * 16)
        for chunk in range(chunks):
            scratch[rows, chunk * LANES : (chunk + 1) * LANES] = in_ref[chunk, rows, :].astype(F32)
        copy = pltpu.make_async_copy(scratch.at[rows], out_ref.at[rows], sent.at[part])
        copy.start()
        copies.append(copy)
    for copy in copies:
        copy.wait()


def per_device(light_field, channel_weights):
    group = ("crow", "ccol")
    chunks = lax.axis_size(group)
    bands = lax.axis_size("band")
    params = lambda mib: pltpu.CompilerParams(vmem_limit_bytes=mib * MIB)
    vmem = pl.BlockSpec(memory_space=pltpu.VMEM)
    hbm = pl.BlockSpec(memory_space=pl.ANY)

    packed = pl.pallas_call(
        functools.partial(gray_kernel, chunks),
        in_specs=[hbm, hbm],
        out_specs=vmem,
        out_shape=jax.ShapeDtypeStruct((chunks, 136, LANES), BF16),
        scratch_shapes=[
            pltpu.VMEM((8, 4, 16, chunks * LANES), BF16),
            pltpu.VMEM((chunks + 2, 16, LANES), F32),
            pltpu.SMEM((4,), F32),
            pltpu.SemaphoreType.DMA((8,)),
            pltpu.SemaphoreType.DMA,
        ],
        compiler_params=params(58),
        name="gray",
    )(channel_weights, light_field)
    columns = lax.all_to_all(packed, group, 0, 0, tiled=True).reshape(8, 4, 136, LANES)

    first, final = pl.pallas_call(
        edges_kernel,
        in_specs=[vmem],
        out_specs=[vmem, vmem],
        out_shape=[jax.ShapeDtypeStruct((3, 16, 16, LANES), BF16)] * 2,
        scratch_shapes=[pltpu.VMEM((16, 16 * PITCH, LANES), F32)],
        compiler_params=params(16),
        name="edges",
    )(columns)
    low = lax.ppermute(final, "band", [(n, n + 1) for n in range(bands - 1)])
    high = lax.ppermute(first, "band", [(n + 1, n) for n in range(bands - 1)])

    hor, gray, inner = pl.pallas_call(
        inner_kernel,
        in_specs=[vmem],
        out_specs=[vmem, vmem, vmem],
        out_shape=[
            jax.ShapeDtypeStruct((3, 16, 16 * PITCH, LANES), F32),
            jax.ShapeDtypeStruct((16, 16, 16, LANES), F32),
            jax.ShapeDtypeStruct((16, 16 * PITCH, LANES), F32),
        ],
        scratch_shapes=[
            pltpu.VMEM((2, 256, LANES), BF16),
            pltpu.VMEM((3, 2, 256, LANES), BF16),
            pltpu.VMEM((8, 256, LANES), BF16),
            pltpu.VMEM((8, 256, LANES), BF16),
            pltpu.VMEM((16, 16 * PITCH, LANES), F32),
            pltpu.VMEM((3, 16, 10, 16, LANES), F32),
        ],
        compiler_params=params(28),
        cost_estimate=pl.CostEstimate(flops=10**9, bytes_accessed=8 * MIB, transcendentals=0),
        name="inner",
    )(columns)

    depth = pl.pallas_call(
        outer_kernel,
        in_specs=[vmem] * 5,
        out_specs=vmem,
        out_shape=jax.ShapeDtypeStruct((8, 4, 2, 64, LANES), BF16),
        scratch_shapes=[
            pltpu.VMEM((3, 16, 6, 16, LANES), F32),
            pltpu.VMEM((16, 16 * PITCH, LANES), F32),
        ],
        compiler_params=params(28),
        name="outer",
    )(gray, low, high, hor, inner)

    back = lax.all_to_all(depth.reshape(chunks, 128, LANES), group, 0, 0, tiled=True)
    out = pl.pallas_call(
        functools.partial(spread_kernel, chunks),
        in_specs=[vmem],
        out_specs=hbm,
        out_shape=jax.ShapeDtypeStruct((128, chunks * LANES), F32),
        scratch_shapes=[pltpu.VMEM((128, chunks * LANES), F32), pltpu.SemaphoreType.DMA((8,))],
        compiler_params=params(8),
        name="spread",
    )(back)
    return out.reshape(2, 4, 16, chunks * LANES)


def solution(mesh):
    placed = (P(None, "crow", "ccol", "band", None), P())
    return jax.shard_map(
        per_device,
        mesh=mesh,
        in_specs=placed,
        out_specs=P("crow", "ccol", "band", None),
        check_vma=False,
    )
```

```python
import functools

import jax
import jax.numpy as jnp
from jax import lax
from jax.experimental import pallas as pl
from jax.experimental.pallas import tpu as pltpu
from jax.sharding import PartitionSpec as P

F32, BF16 = jnp.float32, jnp.bfloat16
LANES = 128
MIB = 1 << 20
NT = (((1,), (1,)), ((), ()))


def iota(shape, dim):
    return lax.broadcasted_iota(jnp.int32, shape, dim)


def ones_where(*conditions_and_values):
    total = None
    for condition, value in conditions_and_values:
        term = jnp.where(condition, F32(value), F32(0.0))
        total = term if total is None else total + term
    return total


PIECE = 4


def gray_kernel(chunks, weights_hbm, field_ref, out_ref, field, packed, weights_ref, arrived, sent, known):
    weights_copy = pltpu.make_async_copy(weights_hbm, weights_ref, known)
    weights_copy.start()
    pieces = chunks // PIECE
    copies = []
    for piece in range(pieces):
        lanes = pl.ds(piece * PIECE * LANES, PIECE * LANES)
        copies.append(
            pltpu.make_async_copy(
                field_ref.at[:, :, :, :, lanes], field.at[piece], arrived.at[piece]
            )
        )
        copies[-1].start()
    row, lane = iota((16, LANES), 0), iota((16, LANES), 1)
    wanted = jnp.where(row < 3, row + 125, jnp.where(row == 3, 0, jnp.where(row == 4, 127, row - 5)))
    select = jnp.where((row < 8) & (lane == wanted), F32(1.0), F32(0.0)).astype(BF16)
    low, middle = row < 3, row < 5
    weights_copy.wait()
    weights = [weights_ref[channel] for channel in range(4)]
    edges = [jnp.zeros((16, LANES), F32)]
    leaving, done = [], 0
    for piece in range(pieces):
        copies[piece].wait()
        for local in range(PIECE):
            chunk = piece * PIECE + local
            lanes = slice(local * LANES, (local + 1) * LANES)
            levels = []
            for cam in range(8):
                total = field[piece, 0, cam // 4, cam % 4, :, lanes].astype(F32) * weights[0]
                for channel in range(1, 4):
                    value = field[piece, channel, cam // 4, cam % 4, :, lanes]
                    total = total + value.astype(F32) * weights[channel]
                levels.append(total.astype(BF16))
            levels = jnp.concatenate(levels)
            packed[chunk, 0:128, :] = levels
            edges.append(lax.dot_general(select, levels, NT, preferred_element_type=F32))
        if piece == pieces - 1:
            edges.append(edges[0])
        ready = len(edges) - 2
        for chunk in range(done, ready):
            left, own, right = edges[chunk : chunk + 3]
            halo = jnp.where(low, left, jnp.where(middle, own, right))
            packed[chunk, 128:136, :] = halo[0:8].astype(BF16)
        part = pl.ds(done, ready - done)
        leaving.append(pltpu.make_async_copy(packed.at[part], out_ref.at[part], sent.at[piece]))
        leaving[-1].start()
        done = ready
    for copy in leaving:
        copy.wait()


PITCH = 17


def is_first_core():
    return lax.rem(lax.axis_index("ccol"), 2) == 0


def edges_kernel(in_ref, up_ref, down_ref, scratch):
    up = jnp.where(is_first_core(), 13, 0)
    down = 13 - up
    for c in range(8):
        for i in range(2):
            s = c * 2 + i
            for t in range(16):
                rows = slice(i * 64 + t % 4 * 16, i * 64 + t % 4 * 16 + 16)
                scratch[s, t * PITCH : t * PITCH + 16, :] = in_ref[c, t // 4, rows, :].astype(F32)
            for r in range(3):
                up_ref[r, s] = scratch[s, pl.ds(r + up, 16, stride=PITCH), :].astype(BF16)
                down_ref[r, s] = scratch[s, pl.ds(r + down, 16, stride=PITCH), :].astype(BF16)


class Smoother:
    def __init__(self):
        self.last = [None] * 4

    def push(self, value):
        for n in range(4):
            before, self.last[n] = self.last[n], value
            if before is not None:
                value = before if value is None else value + before
        return value


def tensor_of_cameras(field, grad_img):
    count = len(field)
    smoothers = [Smoother() for _ in range(3)]
    result = [[] for _ in range(3)]
    for t in range(count + 2):
        products = (None,) * 3
        if t < count:
            if t == 0:
                grad_cam = -field[1]
            elif t == count - 1:
                grad_cam = field[t - 1]
            else:
                grad_cam = field[t - 1] - field[t + 1]
            products = (grad_cam * grad_cam, grad_cam * grad_img[t], grad_img[t] * grad_img[t])
        for f in range(3):
            value = smoothers[f].push(products[f])
            if t >= 2:
                result[f].append(value.astype(BF16))
    return result


def split(values):
    return [values[n * 16 : (n + 1) * 16] for n in range(values.shape[0] // 16)]


def products_of(field, s, r, factor=None):
    if s == 0:
        grad_cam = -field(1, r)
    elif s == 15:
        grad_cam = field(14, r)
    else:
        grad_cam = field(s - 1, r) - field(s + 1, r)
    grad_img = field(s, r + 1) - field(s, r - 1)
    if factor is not None:
        grad_img = grad_img * factor
    return grad_cam * grad_cam, grad_cam * grad_img, grad_img * grad_img


def merge_rows(rows, sums, hor_ref, depth_ref):
    for n, r in enumerate(rows):
        smoothers = [Smoother() for _ in range(3)]
        lines = pl.ds(r, 16, stride=PITCH)
        for s in range(18):
            vertical = [smoothers[f].push(sums[f, s, n] if s < 16 else None) for f in range(3)]
            if s >= 2:
                horizontal = [hor_ref[f, s - 2, lines, :] for f in range(3)]
                depth_ref[s - 2, lines, :] = merge(horizontal, vertical)


def matrices_kernel(grads, smooths):
    k, u = iota((LANES, LANES), 0), iota((LANES, LANES), 1)
    d = k - u
    dist = jnp.abs(d)
    group = ("crow", "ccol")
    place, last = lax.axis_index(group), lax.axis_size(group) - 1
    unit = 1.0 / 1024.0
    has_left = jnp.where(place > 0, F32(unit), F32(0.0))
    has_right = jnp.where(place < last, F32(unit), F32(0.0))
    h, col = iota((8, LANES), 0), iota((8, LANES), 1)
    grad_edge = ones_where(((h == 2) & (col == 0), -1.0), ((h == 5) & (col == 127), 1.0))
    left = ones_where(
        ((h == 1) & (col == 0), 1.0), ((h == 2) & (col == 0), 4.0), ((h == 2) & (col == 1), 1.0)
    )
    right = ones_where(
        ((h == 5) & (col == 127), 4.0),
        ((h == 5) & (col == 126), 1.0),
        ((h == 6) & (col == 127), 1.0),
    )
    smooth_edge = left * has_left + right * has_right
    grad_own = ones_where((d == 1, 1.0), (d == -1, -1.0)).astype(BF16)
    smooth_own = ones_where(
        (dist == 0, 6.0 * unit), (dist == 1, 4.0 * unit), (dist == 2, unit)
    ).astype(BF16)
    zero = jnp.zeros((8, LANES), F32)
    for c in range(8):
        for matrix, own, side in ((grads, grad_own, grad_edge), (smooths, smooth_own, smooth_edge)):
            matrix[c, 0:128, :] = own
            for n in range(8):
                pair = [side if n * 2 + m == c else zero for m in range(2)]
                matrix[c, 128 + n * 16 : 144 + n * 16, :] = jnp.concatenate(pair).astype(BF16)


def inner_kernel(
    in_ref, grads, smooths, out_ref, gray_ref, depth_ref, edge, edge_sums, scratch, sums
):
    k, u = iota((LANES, LANES), 0), iota((LANES, LANES), 1)
    d = k - u
    eye = ones_where((d == 0, 1.0)).astype(BF16)
    for col in range(4):
        rows = [in_ref[c, col, 128:136, :].astype(F32) for c in range(8)]
        rows = jnp.concatenate(rows + [jnp.zeros((64, LANES), F32)]).astype(BF16)
        moved = lax.dot_general(eye, rows, NT, preferred_element_type=F32).astype(BF16)
        for i in range(2):
            edge[i, col * 64 : (col + 1) * 64, :] = moved[i * 64 : (i + 1) * 64]
    slot = u & 7
    used = ((k >> 3) == (u >> 3)) & ((slot == 1) | (slot == 2) | (slot == 5) | (slot == 6))
    grad = ones_where((used & (d == 1), 1.0), (used & (d == -1), -1.0)).astype(BF16)
    for i in range(2):
        values = edge[i]
        grad_img = jnp.dot(values, grad, preferred_element_type=F32)
        summed = tensor_of_cameras(split(values.astype(F32)), split(grad_img))
        for f in range(3):
            for t in range(16):
                edge_sums[f, i, t * 16 : (t + 1) * 16, :] = summed[f][t]

    def values_of(c, i):
        return in_ref[c, :, i * 64 : (i + 1) * 64, :].reshape(256, LANES)

    def gradient(c):
        own = jnp.concatenate([values_of(c, 0), values_of(c, 1)])
        side = jnp.concatenate([edge[0], edge[1]])
        return jnp.dot(
            jnp.concatenate([own, side], axis=1), grads[c], preferred_element_type=F32
        )

    def products(c, grad_img):
        summed = []
        for i in range(2):
            field = split(values_of(c, i).astype(F32))
            for t in range(16):
                scratch[c * 2 + i, t * PITCH : t * PITCH + 16, :] = field[t]
            for r in range(16):
                gray_ref[c * 2 + i, r] = scratch[c * 2 + i, pl.ds(r, 16, stride=PITCH), :]
            summed.append(tensor_of_cameras(field, split(grad_img[i * 256 : (i + 1) * 256])))
        return jnp.concatenate([v for f in range(3) for i in range(2) for v in summed[i][f]])

    def smooth(c, parts):
        side = jnp.concatenate([edge_sums[f, i] for f in range(3) for i in range(2)])
        full = jnp.dot(
            jnp.concatenate([parts, side], axis=1), smooths[c], preferred_element_type=F32
        )
        for f in range(3):
            for i in range(2):
                n = (f * 2 + i) * 256
                for t in range(16):
                    rows = slice(t * PITCH, t * PITCH + 16)
                    out_ref[f, c * 2 + i, rows, :] = full[n + t * 16 : n + t * 16 + 16]

    grad_img, parts = gradient(0), None
    for c in range(8):
        following = gradient(c + 1) if c < 7 else None
        now = products(c, grad_img)
        if c:
            smooth(c - 1, parts)
        grad_img, parts = following, now
    smooth(7, parts)

    for s in range(16):
        smoothers = [Smoother() for _ in range(3)]
        for r in range(1, 15):
            products = products_of(lambda s, r: gray_ref[s, r], s, r)
            for f in range(3):
                value = smoothers[f].push(products[f])
                if r >= 5:
                    sums[f, s, r - 5] = value
    merge_rows(range(3, 13), sums, out_ref, depth_ref)


def parts_of(jaa, jab, jbb, scale):
    spread, total = jaa - jbb, jaa + jbb
    twice = jab + jab
    near = F32(0.1 * scale)
    return spread * spread + twice * twice, total * total + near * F32(scale), jab, jbb + near


def merge(horizontal, vertical):
    nh, dh, bh, ah = parts_of(*horizontal, 1.0)
    nv, dv, bv, av = parts_of(*vertical, 1024.0)
    p, q = nh * dv, nv * dh
    top = p * (bh * av) + q * (bv * ah)
    return top / ((p + q + 0.1 * (dh * dv)) * (ah * av))


def outer_kernel(gray_ref, one_ref, two_ref, hor_ref, inner_ref, out_ref, sums, depth, halo):
    band, last = lax.axis_index("band"), lax.axis_size("band") - 1
    has_low = jnp.where(band > 0, F32(1.0), F32(0.0))
    has_high = jnp.where(band < last, F32(1.0), F32(0.0))

    first_core = is_first_core()
    for r in range(3):
        for s in range(16):
            one, two = one_ref[r, s].astype(F32), two_ref[r, s].astype(F32)
            halo[r, s] = jnp.where(first_core, one, two)
            halo[r + 3, s] = jnp.where(first_core, two, one)

    def field(s, r):
        if r < 0:
            return halo[r + 3, s]
        return gray_ref[s, r] if r < 16 else halo[r - 13, s]

    for s in range(16):
        for side in range(2):
            smoothers = [Smoother() for _ in range(3)]
            for q in range(7):
                r = q + 11 if side else q - 2
                factor = has_low if r < 0 else has_high if r >= 16 else None
                products = products_of(field, s, r, factor)
                for f in range(3):
                    value = smoothers[f].push(products[f])
                    if q >= 4:
                        sums[f, s, side * 3 + q - 4] = value
    merge_rows((0, 1, 2, 13, 14, 15), sums, hor_ref, depth)

    row = iota((16, LANES), 0)
    is_inner = (row >= 3) & (row < 13)
    for s in range(16):
        for t in range(16):
            lines = slice(t * PITCH, t * PITCH + 16)
            value = jnp.where(is_inner, inner_ref[s, lines, :], depth[s, lines, :])
            rows = slice(t % 4 * 16, t % 4 * 16 + 16)
            out_ref[s // 2, t // 4, s % 2, rows, :] = value.astype(BF16)


def spread_kernel(chunks, in_ref, out_ref, scratch, sent):
    copies = []
    for part in range(8):
        rows = slice(part * 16, (part + 1) * 16)
        for chunk in range(chunks):
            scratch[rows, chunk * LANES : (chunk + 1) * LANES] = in_ref[chunk, rows, :].astype(F32)
        copy = pltpu.make_async_copy(scratch.at[rows], out_ref.at[rows], sent.at[part])
        copy.start()
        copies.append(copy)
    for copy in copies:
        copy.wait()


def per_device(light_field, channel_weights):
    group = ("crow", "ccol")
    chunks = lax.axis_size(group)
    bands = lax.axis_size("band")
    params = lambda mib: pltpu.CompilerParams(vmem_limit_bytes=mib * MIB)
    vmem = pl.BlockSpec(memory_space=pltpu.VMEM)
    hbm = pl.BlockSpec(memory_space=pl.ANY)

    packed = pl.pallas_call(
        functools.partial(gray_kernel, chunks),
        in_specs=[hbm, hbm],
        out_specs=hbm,
        out_shape=jax.ShapeDtypeStruct((chunks, 136, LANES), BF16),
        scratch_shapes=[
            pltpu.VMEM((chunks // PIECE, 4, 2, 4, 16, PIECE * LANES), BF16),
            pltpu.VMEM((chunks, 136, LANES), BF16),
            pltpu.SMEM((4,), F32),
            pltpu.SemaphoreType.DMA((chunks // PIECE,)),
            pltpu.SemaphoreType.DMA((chunks // PIECE,)),
            pltpu.SemaphoreType.DMA,
        ],
        compiler_params=params(58),
        name="gray",
    )(channel_weights, light_field)
    columns = lax.all_to_all(packed, group, 0, 0, tiled=True).reshape(8, 4, 136, LANES)
    grads, smooths = pl.pallas_call(
        matrices_kernel,
        out_specs=[vmem, vmem],
        out_shape=[jax.ShapeDtypeStruct((8, 256, LANES), BF16)] * 2,
        compiler_params=params(8),
        cost_estimate=pl.CostEstimate(flops=10**9, bytes_accessed=8 * MIB, transcendentals=0),
        name="matrices",
    )()
    columns, grads, smooths = lax.optimization_barrier((columns, grads, smooths))

    ahead, behind = pl.pallas_call(
        edges_kernel,
        in_specs=[vmem],
        out_specs=[vmem, vmem],
        out_shape=[jax.ShapeDtypeStruct((3, 16, 16, LANES), BF16)] * 2,
        scratch_shapes=[pltpu.VMEM((16, 16 * PITCH, LANES), F32)],
        compiler_params=params(16),
        name="edges",
    )(columns)
    pairs = [(k % 2, k * bands + n, k * bands + n + 1) for k in range(4) for n in range(bands - 1)]
    both = ("ccol", "band")
    one = lax.ppermute(ahead, both, [(b, a) if odd else (a, b) for odd, a, b in pairs])
    two = lax.ppermute(behind, both, [(a, b) if odd else (b, a) for odd, a, b in pairs])

    hor, gray, inner = pl.pallas_call(
        inner_kernel,
        in_specs=[vmem, vmem, vmem],
        out_specs=[vmem, vmem, vmem],
        out_shape=[
            jax.ShapeDtypeStruct((3, 16, 16 * PITCH, LANES), F32),
            jax.ShapeDtypeStruct((16, 16, 16, LANES), F32),
            jax.ShapeDtypeStruct((16, 16 * PITCH, LANES), F32),
        ],
        scratch_shapes=[
            pltpu.VMEM((2, 256, LANES), BF16),
            pltpu.VMEM((3, 2, 256, LANES), BF16),
            pltpu.VMEM((16, 16 * PITCH, LANES), F32),
            pltpu.VMEM((3, 16, 10, 16, LANES), F32),
        ],
        compiler_params=params(28),
        cost_estimate=pl.CostEstimate(flops=10**9, bytes_accessed=8 * MIB, transcendentals=0),
        name="inner",
    )(columns, grads, smooths)

    depth = pl.pallas_call(
        outer_kernel,
        in_specs=[vmem] * 5,
        out_specs=vmem,
        out_shape=jax.ShapeDtypeStruct((8, 4, 2, 64, LANES), BF16),
        scratch_shapes=[
            pltpu.VMEM((3, 16, 6, 16, LANES), F32),
            pltpu.VMEM((16, 16 * PITCH, LANES), F32),
            pltpu.VMEM((6, 16, 16, LANES), F32),
        ],
        compiler_params=params(28),
        name="outer",
    )(gray, one, two, hor, inner)

    back = lax.all_to_all(depth.reshape(chunks, 128, LANES), group, 0, 0, tiled=True)
    out = pl.pallas_call(
        functools.partial(spread_kernel, chunks),
        in_specs=[vmem],
        out_specs=hbm,
        out_shape=jax.ShapeDtypeStruct((128, chunks * LANES), F32),
        scratch_shapes=[pltpu.VMEM((128, chunks * LANES), F32), pltpu.SemaphoreType.DMA((8,))],
        compiler_params=params(8),
        name="spread",
    )(back)
    return out.reshape(2, 4, 16, chunks * LANES)


def solution(mesh):
    placed = (P(None, "crow", "ccol", "band", None), P())
    return jax.shard_map(
        per_device,
        mesh=mesh,
        in_specs=placed,
        out_specs=P("crow", "ccol", "band", None),
        check_vma=False,
    )
```

```python
import functools

import jax
import jax.numpy as jnp
from jax import lax
from jax.experimental import pallas as pl
from jax.experimental.pallas import tpu as pltpu
from jax.sharding import PartitionSpec as P

F32, BF16 = jnp.float32, jnp.bfloat16
LANES = 128
MIB = 1 << 20
NT = (((1,), (1,)), ((), ()))


def iota(shape, dim):
    return lax.broadcasted_iota(jnp.int32, shape, dim)


def ones_where(*conditions_and_values):
    total = None
    for condition, value in conditions_and_values:
        term = jnp.where(condition, F32(value), F32(0.0))
        total = term if total is None else total + term
    return total


PIECE = 4


def gray_kernel(chunks, weights_hbm, field_ref, out_ref, field, packed, weights_ref, arrived, sent, known):
    weights_copy = pltpu.make_async_copy(weights_hbm, weights_ref, known)
    weights_copy.start()
    pieces = chunks // PIECE
    copies = []
    for piece in range(pieces):
        lanes = pl.ds(piece * PIECE * LANES, PIECE * LANES)
        copies.append(
            pltpu.make_async_copy(
                field_ref.at[:, :, :, :, lanes], field.at[piece], arrived.at[piece]
            )
        )
        copies[-1].start()
    row, lane = iota((16, LANES), 0), iota((16, LANES), 1)
    wanted = jnp.where(row < 3, row + 125, jnp.where(row == 3, 0, jnp.where(row == 4, 127, row - 5)))
    select = jnp.where((row < 8) & (lane == wanted), F32(1.0), F32(0.0)).astype(BF16)
    low, middle = row < 3, row < 5
    weights_copy.wait()
    weights = [weights_ref[channel] for channel in range(4)]
    edges = [jnp.zeros((16, LANES), F32)]
    leaving, done = [], 0
    for piece in range(pieces):
        copies[piece].wait()
        for local in range(PIECE):
            chunk = piece * PIECE + local
            lanes = slice(local * LANES, (local + 1) * LANES)
            levels = []
            for cam in range(8):
                total = field[piece, 0, cam // 4, cam % 4, :, lanes].astype(F32) * weights[0]
                for channel in range(1, 4):
                    value = field[piece, channel, cam // 4, cam % 4, :, lanes]
                    total = total + value.astype(F32) * weights[channel]
                levels.append(total.astype(BF16))
            levels = jnp.concatenate(levels)
            packed[chunk, 0:128, :] = levels
            edges.append(lax.dot_general(select, levels, NT, preferred_element_type=F32))
        if piece == pieces - 1:
            edges.append(edges[0])
        ready = len(edges) - 2
        for chunk in range(done, ready):
            left, own, right = edges[chunk : chunk + 3]
            halo = jnp.where(low, left, jnp.where(middle, own, right))
            packed[chunk, 128:136, :] = halo[0:8].astype(BF16)
        part = pl.ds(done, ready - done)
        leaving.append(pltpu.make_async_copy(packed.at[part], out_ref.at[part], sent.at[piece]))
        leaving[-1].start()
        done = ready
    for copy in leaving:
        copy.wait()


PITCH = 17


def is_even_band():
    return lax.rem(lax.axis_index("band"), 2) == 0


def edges_kernel(in_ref, up_ref, down_ref, scratch):
    up = jnp.where(is_even_band(), 13, 0)
    down = 13 - up
    for c in range(8):
        for i in range(2):
            s = c * 2 + i
            for t in range(16):
                rows = slice(i * 64 + t % 4 * 16, i * 64 + t % 4 * 16 + 16)
                scratch[s, t * PITCH : t * PITCH + 16, :] = in_ref[c, t // 4, rows, :].astype(F32)
            for r in range(3):
                up_ref[r, s] = scratch[s, pl.ds(r + up, 16, stride=PITCH), :].astype(BF16)
                down_ref[r, s] = scratch[s, pl.ds(r + down, 16, stride=PITCH), :].astype(BF16)


class Smoother:
    def __init__(self):
        self.last = [None] * 4

    def push(self, value):
        for n in range(4):
            before, self.last[n] = self.last[n], value
            if before is not None:
                value = before if value is None else value + before
        return value


def tensor_of_cameras(field, grad_img):
    count = len(field)
    smoothers = [Smoother() for _ in range(3)]
    result = [[] for _ in range(3)]
    for t in range(count + 2):
        products = (None,) * 3
        if t < count:
            if t == 0:
                grad_cam = -field[1]
            elif t == count - 1:
                grad_cam = field[t - 1]
            else:
                grad_cam = field[t - 1] - field[t + 1]
            products = (grad_cam * grad_cam, grad_cam * grad_img[t], grad_img[t] * grad_img[t])
        for f in range(3):
            value = smoothers[f].push(products[f])
            if t >= 2:
                result[f].append(value.astype(BF16))
    return result


def split(values):
    return [values[n * 16 : (n + 1) * 16] for n in range(values.shape[0] // 16)]


def products_of(field, s, r, factor=None):
    if s == 0:
        grad_cam = -field(1, r)
    elif s == 15:
        grad_cam = field(14, r)
    else:
        grad_cam = field(s - 1, r) - field(s + 1, r)
    grad_img = field(s, r + 1) - field(s, r - 1)
    if factor is not None:
        grad_img = grad_img * factor
    return grad_cam * grad_cam, grad_cam * grad_img, grad_img * grad_img


def merge_rows(rows, sums, hor_ref, depth_ref):
    for n, r in enumerate(rows):
        smoothers = [Smoother() for _ in range(3)]
        lines = pl.ds(r, 16, stride=PITCH)
        for s in range(18):
            vertical = [smoothers[f].push(sums[f, s, n] if s < 16 else None) for f in range(3)]
            if s >= 2:
                horizontal = [hor_ref[f, s - 2, lines, :] for f in range(3)]
                depth_ref[s - 2, lines, :] = merge(horizontal, vertical)


def matrices_kernel(grads, smooths):
    k, u = iota((LANES, LANES), 0), iota((LANES, LANES), 1)
    d = k - u
    dist = jnp.abs(d)
    group = ("crow", "ccol")
    place, last = lax.axis_index(group), lax.axis_size(group) - 1
    unit = 1.0 / 1024.0
    has_left = jnp.where(place > 0, F32(unit), F32(0.0))
    has_right = jnp.where(place < last, F32(unit), F32(0.0))
    h, col = iota((8, LANES), 0), iota((8, LANES), 1)
    grad_edge = ones_where(((h == 2) & (col == 0), -1.0), ((h == 5) & (col == 127), 1.0))
    left = ones_where(
        ((h == 1) & (col == 0), 1.0), ((h == 2) & (col == 0), 4.0), ((h == 2) & (col == 1), 1.0)
    )
    right = ones_where(
        ((h == 5) & (col == 127), 4.0),
        ((h == 5) & (col == 126), 1.0),
        ((h == 6) & (col == 127), 1.0),
    )
    smooth_edge = left * has_left + right * has_right
    grad_own = ones_where((d == 1, 1.0), (d == -1, -1.0)).astype(BF16)
    smooth_own = ones_where(
        (dist == 0, 6.0 * unit), (dist == 1, 4.0 * unit), (dist == 2, unit)
    ).astype(BF16)
    zero = jnp.zeros((8, LANES), F32)
    for c in range(8):
        for matrix, own, side in ((grads, grad_own, grad_edge), (smooths, smooth_own, smooth_edge)):
            matrix[c, 0:128, :] = own
            for n in range(8):
                pair = [side if n * 2 + m == c else zero for m in range(2)]
                matrix[c, 128 + n * 16 : 144 + n * 16, :] = jnp.concatenate(pair).astype(BF16)


def inner_kernel(
    in_ref, grads, smooths, out_ref, gray_ref, depth_ref, edge, edge_sums, scratch, sums
):
    k, u = iota((LANES, LANES), 0), iota((LANES, LANES), 1)
    d = k - u
    eye = ones_where((d == 0, 1.0)).astype(BF16)
    for col in range(4):
        rows = [in_ref[c, col, 128:136, :].astype(F32) for c in range(8)]
        rows = jnp.concatenate(rows + [jnp.zeros((64, LANES), F32)]).astype(BF16)
        moved = lax.dot_general(eye, rows, NT, preferred_element_type=F32).astype(BF16)
        for i in range(2):
            edge[i, col * 64 : (col + 1) * 64, :] = moved[i * 64 : (i + 1) * 64]
    slot = u & 7
    used = ((k >> 3) == (u >> 3)) & ((slot == 1) | (slot == 2) | (slot == 5) | (slot == 6))
    grad = ones_where((used & (d == 1), 1.0), (used & (d == -1), -1.0)).astype(BF16)
    for i in range(2):
        values = edge[i]
        grad_img = jnp.dot(values, grad, preferred_element_type=F32)
        summed = tensor_of_cameras(split(values.astype(F32)), split(grad_img))
        for f in range(3):
            for t in range(16):
                edge_sums[f, i, t * 16 : (t + 1) * 16, :] = summed[f][t]

    def values_of(c, i):
        return in_ref[c, :, i * 64 : (i + 1) * 64, :].reshape(256, LANES)

    def gradient(c):
        own = jnp.concatenate([values_of(c, 0), values_of(c, 1)])
        side = jnp.concatenate([edge[0], edge[1]])
        return jnp.dot(
            jnp.concatenate([own, side], axis=1), grads[c], preferred_element_type=F32
        )

    def products(c, grad_img):
        summed = []
        for i in range(2):
            field = split(values_of(c, i).astype(F32))
            for t in range(16):
                scratch[c * 2 + i, t * PITCH : t * PITCH + 16, :] = field[t]
            for r in range(16):
                gray_ref[c * 2 + i, r] = scratch[c * 2 + i, pl.ds(r, 16, stride=PITCH), :]
            summed.append(tensor_of_cameras(field, split(grad_img[i * 256 : (i + 1) * 256])))
        return jnp.concatenate([v for f in range(3) for i in range(2) for v in summed[i][f]])

    def smooth(c, parts):
        side = jnp.concatenate([edge_sums[f, i] for f in range(3) for i in range(2)])
        full = jnp.dot(
            jnp.concatenate([parts, side], axis=1), smooths[c], preferred_element_type=F32
        )
        for f in range(3):
            for i in range(2):
                n = (f * 2 + i) * 256
                for t in range(16):
                    rows = slice(t * PITCH, t * PITCH + 16)
                    out_ref[f, c * 2 + i, rows, :] = full[n + t * 16 : n + t * 16 + 16]

    grad_img, parts = gradient(0), None
    for c in range(8):
        following = gradient(c + 1) if c < 7 else None
        now = products(c, grad_img)
        if c:
            smooth(c - 1, parts)
        grad_img, parts = following, now
    smooth(7, parts)

    for s in range(16):
        smoothers = [Smoother() for _ in range(3)]
        for r in range(1, 15):
            products = products_of(lambda s, r: gray_ref[s, r], s, r)
            for f in range(3):
                value = smoothers[f].push(products[f])
                if r >= 5:
                    sums[f, s, r - 5] = value
    merge_rows(range(3, 13), sums, out_ref, depth_ref)


def parts_of(jaa, jab, jbb, scale):
    spread, total = jaa - jbb, jaa + jbb
    twice = jab + jab
    near = F32(0.1 * scale)
    return spread * spread + twice * twice, total * total + near * F32(scale), jab, jbb + near


def merge(horizontal, vertical):
    nh, dh, bh, ah = parts_of(*horizontal, 1.0)
    nv, dv, bv, av = parts_of(*vertical, 1024.0)
    p, q = nh * dv, nv * dh
    top = p * (bh * av) + q * (bv * ah)
    return top / ((p + q + 0.1 * (dh * dv)) * (ah * av))


def outer_kernel(gray_ref, one_ref, two_ref, hor_ref, inner_ref, out_ref, sums, depth, halo):
    band, last = lax.axis_index("band"), lax.axis_size("band") - 1
    has_low = jnp.where(band > 0, F32(1.0), F32(0.0))
    has_high = jnp.where(band < last, F32(1.0), F32(0.0))

    even = is_even_band()
    for r in range(3):
        for s in range(16):
            one, two = one_ref[r, s].astype(F32), two_ref[r, s].astype(F32)
            halo[r, s] = jnp.where(even, two, one)
            halo[r + 3, s] = jnp.where(even, one, two)

    def field(s, r):
        if r < 0:
            return halo[r + 3, s]
        return gray_ref[s, r] if r < 16 else halo[r - 13, s]

    for s in range(16):
        for side in range(2):
            smoothers = [Smoother() for _ in range(3)]
            for q in range(7):
                r = q + 11 if side else q - 2
                factor = has_low if r < 0 else has_high if r >= 16 else None
                products = products_of(field, s, r, factor)
                for f in range(3):
                    value = smoothers[f].push(products[f])
                    if q >= 4:
                        sums[f, s, side * 3 + q - 4] = value
    merge_rows((0, 1, 2, 13, 14, 15), sums, hor_ref, depth)

    row = iota((16, LANES), 0)
    is_inner = (row >= 3) & (row < 13)
    for s in range(16):
        for t in range(16):
            lines = slice(t * PITCH, t * PITCH + 16)
            value = jnp.where(is_inner, inner_ref[s, lines, :], depth[s, lines, :])
            rows = slice(t % 4 * 16, t % 4 * 16 + 16)
            out_ref[s // 2, t // 4, s % 2, rows, :] = value.astype(BF16)


def spread_kernel(chunks, in_ref, out_ref, scratch, sent):
    copies = []
    for part in range(8):
        rows = slice(part * 16, (part + 1) * 16)
        for chunk in range(chunks):
            scratch[rows, chunk * LANES : (chunk + 1) * LANES] = in_ref[chunk, rows, :].astype(F32)
        copy = pltpu.make_async_copy(scratch.at[rows], out_ref.at[rows], sent.at[part])
        copy.start()
        copies.append(copy)
    for copy in copies:
        copy.wait()


def per_device(light_field, channel_weights):
    group = ("crow", "ccol")
    chunks = lax.axis_size(group)
    bands = lax.axis_size("band")
    params = lambda mib: pltpu.CompilerParams(vmem_limit_bytes=mib * MIB)
    vmem = pl.BlockSpec(memory_space=pltpu.VMEM)
    hbm = pl.BlockSpec(memory_space=pl.ANY)

    packed = pl.pallas_call(
        functools.partial(gray_kernel, chunks),
        in_specs=[hbm, hbm],
        out_specs=hbm,
        out_shape=jax.ShapeDtypeStruct((chunks, 136, LANES), BF16),
        scratch_shapes=[
            pltpu.VMEM((chunks // PIECE, 4, 2, 4, 16, PIECE * LANES), BF16),
            pltpu.VMEM((chunks, 136, LANES), BF16),
            pltpu.SMEM((4,), F32),
            pltpu.SemaphoreType.DMA((chunks // PIECE,)),
            pltpu.SemaphoreType.DMA((chunks // PIECE,)),
            pltpu.SemaphoreType.DMA,
        ],
        compiler_params=params(58),
        name="gray",
    )(channel_weights, light_field)
    columns = lax.all_to_all(packed, group, 0, 0, tiled=True).reshape(8, 4, 136, LANES)
    grads, smooths = pl.pallas_call(
        matrices_kernel,
        out_specs=[vmem, vmem],
        out_shape=[jax.ShapeDtypeStruct((8, 256, LANES), BF16)] * 2,
        compiler_params=params(8),
        cost_estimate=pl.CostEstimate(flops=10**9, bytes_accessed=8 * MIB, transcendentals=0),
        name="matrices",
    )()
    columns, grads, smooths = lax.optimization_barrier((columns, grads, smooths))

    ahead, behind = pl.pallas_call(
        edges_kernel,
        in_specs=[vmem],
        out_specs=[vmem, vmem],
        out_shape=[jax.ShapeDtypeStruct((3, 16, 16, LANES), BF16)] * 2,
        scratch_shapes=[pltpu.VMEM((16, 16 * PITCH, LANES), F32)],
        compiler_params=params(16),
        name="edges",
    )(columns)
    links = [[(n, n + 1) for n in range(start, bands - 1, 2)] for start in range(2)]
    one, two = (
        lax.ppermute(rows, "band", pairs + [(b, a) for a, b in pairs])
        for rows, pairs in zip((ahead, behind), links)
    )

    hor, gray, inner = pl.pallas_call(
        inner_kernel,
        in_specs=[vmem, vmem, vmem],
        out_specs=[vmem, vmem, vmem],
        out_shape=[
            jax.ShapeDtypeStruct((3, 16, 16 * PITCH, LANES), F32),
            jax.ShapeDtypeStruct((16, 16, 16, LANES), F32),
            jax.ShapeDtypeStruct((16, 16 * PITCH, LANES), F32),
        ],
        scratch_shapes=[
            pltpu.VMEM((2, 256, LANES), BF16),
            pltpu.VMEM((3, 2, 256, LANES), BF16),
            pltpu.VMEM((16, 16 * PITCH, LANES), F32),
            pltpu.VMEM((3, 16, 10, 16, LANES), F32),
        ],
        compiler_params=params(28),
        cost_estimate=pl.CostEstimate(flops=10**9, bytes_accessed=8 * MIB, transcendentals=0),
        name="inner",
    )(columns, grads, smooths)

    depth = pl.pallas_call(
        outer_kernel,
        in_specs=[vmem] * 5,
        out_specs=vmem,
        out_shape=jax.ShapeDtypeStruct((8, 4, 2, 64, LANES), BF16),
        scratch_shapes=[
            pltpu.VMEM((3, 16, 6, 16, LANES), F32),
            pltpu.VMEM((16, 16 * PITCH, LANES), F32),
            pltpu.VMEM((6, 16, 16, LANES), F32),
        ],
        compiler_params=params(28),
        name="outer",
    )(gray, one, two, hor, inner)

    back = lax.all_to_all(depth.reshape(chunks, 128, LANES), group, 0, 0, tiled=True)
    out = pl.pallas_call(
        functools.partial(spread_kernel, chunks),
        in_specs=[vmem],
        out_specs=hbm,
        out_shape=jax.ShapeDtypeStruct((128, chunks * LANES), F32),
        scratch_shapes=[pltpu.VMEM((128, chunks * LANES), F32), pltpu.SemaphoreType.DMA((8,))],
        compiler_params=params(8),
        name="spread",
    )(back)
    return out.reshape(2, 4, 16, chunks * LANES)


def solution(mesh):
    placed = (P(None, "crow", "ccol", "band", None), P())
    return jax.shard_map(
        per_device,
        mesh=mesh,
        in_specs=placed,
        out_specs=P("crow", "ccol", "band", None),
        check_vma=False,
    )
```

```python
import functools

import jax
import jax.numpy as jnp
from jax import lax
from jax.experimental import pallas as pl
from jax.experimental.pallas import tpu as pltpu
from jax.sharding import PartitionSpec as P

F32, BF16 = jnp.float32, jnp.bfloat16
LANES = 128
MIB = 1 << 20
NT = (((1,), (1,)), ((), ()))


def iota(shape, dim):
    return lax.broadcasted_iota(jnp.int32, shape, dim)


def ones_where(*conditions_and_values):
    total = None
    for condition, value in conditions_and_values:
        term = jnp.where(condition, F32(value), F32(0.0))
        total = term if total is None else total + term
    return total


PIECE = 4


def gray_kernel(chunks, weights_hbm, field_ref, out_ref, field, packed, weights_ref, arrived, sent, known):
    weights_copy = pltpu.make_async_copy(weights_hbm, weights_ref, known)
    weights_copy.start()
    pieces = chunks // PIECE
    copies = []
    for piece in range(pieces):
        lanes = pl.ds(piece * PIECE * LANES, PIECE * LANES)
        copies.append(
            pltpu.make_async_copy(
                field_ref.at[:, :, :, :, lanes], field.at[piece], arrived.at[piece]
            )
        )
        copies[-1].start()
    row, lane = iota((16, LANES), 0), iota((16, LANES), 1)
    wanted = jnp.where(row < 3, row + 125, jnp.where(row == 3, 0, jnp.where(row == 4, 127, row - 5)))
    select = jnp.where((row < 8) & (lane == wanted), F32(1.0), F32(0.0)).astype(BF16)
    low, middle = row < 3, row < 5
    weights_copy.wait()
    weights = [weights_ref[channel] for channel in range(4)]
    edges = [jnp.zeros((16, LANES), F32)]
    leaving, done = [], 0
    for piece in range(pieces):
        copies[piece].wait()
        for local in range(PIECE):
            chunk = piece * PIECE + local
            lanes = slice(local * LANES, (local + 1) * LANES)
            levels = []
            for cam in range(8):
                total = field[piece, 0, cam // 4, cam % 4, :, lanes].astype(F32) * weights[0]
                for channel in range(1, 4):
                    value = field[piece, channel, cam // 4, cam % 4, :, lanes]
                    total = total + value.astype(F32) * weights[channel]
                levels.append(total.astype(BF16))
            levels = jnp.concatenate(levels)
            packed[chunk, 0:128, :] = levels
            edges.append(lax.dot_general(select, levels, NT, preferred_element_type=F32))
        if piece == pieces - 1:
            edges.append(edges[0])
        ready = len(edges) - 2
        for chunk in range(done, ready):
            left, own, right = edges[chunk : chunk + 3]
            halo = jnp.where(low, left, jnp.where(middle, own, right))
            packed[chunk, 128:136, :] = halo[0:8].astype(BF16)
        part = pl.ds(done, ready - done)
        leaving.append(pltpu.make_async_copy(packed.at[part], out_ref.at[part], sent.at[piece]))
        leaving[-1].start()
        done = ready
    for copy in leaving:
        copy.wait()


PITCH = 17


def is_even_band():
    return lax.rem(lax.axis_index("band"), 2) == 0


def edges_kernel(in_ref, up_ref, down_ref, scratch):
    up = jnp.where(is_even_band(), 13, 0)
    down = 13 - up
    for c in range(8):
        for i in range(2):
            s = c * 2 + i
            for t in range(16):
                rows = slice(i * 64 + t % 4 * 16, i * 64 + t % 4 * 16 + 16)
                scratch[s, t * PITCH : t * PITCH + 16, :] = in_ref[c, t // 4, rows, :].astype(F32)
            for r in range(3):
                up_ref[r, s] = scratch[s, pl.ds(r + up, 16, stride=PITCH), :].astype(BF16)
                down_ref[r, s] = scratch[s, pl.ds(r + down, 16, stride=PITCH), :].astype(BF16)


class Smoother:
    def __init__(self):
        self.last = [None] * 4

    def push(self, value):
        for n in range(4):
            before, self.last[n] = self.last[n], value
            if before is not None:
                value = before if value is None else value + before
        return value


def tensor_of_cameras(field, grad_img):
    count = len(field)
    smoothers = [Smoother() for _ in range(3)]
    result = [[] for _ in range(3)]
    for t in range(count + 2):
        products = (None,) * 3
        if t < count:
            if t == 0:
                grad_cam = -field[1]
            elif t == count - 1:
                grad_cam = field[t - 1]
            else:
                grad_cam = field[t - 1] - field[t + 1]
            products = (grad_cam * grad_cam, grad_cam * grad_img[t], grad_img[t] * grad_img[t])
        for f in range(3):
            value = smoothers[f].push(products[f])
            if t >= 2:
                result[f].append(value.astype(BF16))
    return result


def split(values):
    return [values[n * 16 : (n + 1) * 16] for n in range(values.shape[0] // 16)]


def products_of(field, s, r, factor=None):
    if s == 0:
        grad_cam = -field(1, r)
    elif s == 15:
        grad_cam = field(14, r)
    else:
        grad_cam = field(s - 1, r) - field(s + 1, r)
    grad_img = field(s, r + 1) - field(s, r - 1)
    if factor is not None:
        grad_img = grad_img * factor
    return grad_cam * grad_cam, grad_cam * grad_img, grad_img * grad_img


def merge_rows(rows, sums, hor_ref, depth_ref):
    for n, r in enumerate(rows):
        smoothers = [Smoother() for _ in range(3)]
        lines = pl.ds(r, 16, stride=PITCH)
        for s in range(18):
            vertical = [smoothers[f].push(sums[f, s, n] if s < 16 else None) for f in range(3)]
            if s >= 2:
                horizontal = [hor_ref[f, s - 2, lines, :] for f in range(3)]
                depth_ref[s - 2, lines, :] = merge(horizontal, vertical)


def matrices_kernel(grads, smooths):
    k, u = iota((LANES, LANES), 0), iota((LANES, LANES), 1)
    d = k - u
    dist = jnp.abs(d)
    group = ("crow", "ccol")
    place, last = lax.axis_index(group), lax.axis_size(group) - 1
    unit = 1.0 / 1024.0
    has_left = jnp.where(place > 0, F32(unit), F32(0.0))
    has_right = jnp.where(place < last, F32(unit), F32(0.0))
    h, col = iota((8, LANES), 0), iota((8, LANES), 1)
    grad_edge = ones_where(((h == 2) & (col == 0), -1.0), ((h == 5) & (col == 127), 1.0))
    left = ones_where(
        ((h == 1) & (col == 0), 1.0), ((h == 2) & (col == 0), 4.0), ((h == 2) & (col == 1), 1.0)
    )
    right = ones_where(
        ((h == 5) & (col == 127), 4.0),
        ((h == 5) & (col == 126), 1.0),
        ((h == 6) & (col == 127), 1.0),
    )
    smooth_edge = left * has_left + right * has_right
    grad_own = ones_where((d == 1, 1.0), (d == -1, -1.0)).astype(BF16)
    smooth_own = ones_where(
        (dist == 0, 6.0 * unit), (dist == 1, 4.0 * unit), (dist == 2, unit)
    ).astype(BF16)
    zero = jnp.zeros((8, LANES), F32)
    for c in range(8):
        for matrix, own, side in ((grads, grad_own, grad_edge), (smooths, smooth_own, smooth_edge)):
            matrix[c, 0:128, :] = own
            for n in range(8):
                pair = [side if n * 2 + m == c else zero for m in range(2)]
                matrix[c, 128 + n * 16 : 144 + n * 16, :] = jnp.concatenate(pair).astype(BF16)


def inner_kernel(
    in_ref, grads, smooths, out_ref, gray_ref, depth_ref, edge, edge_sums, scratch, sums
):
    k, u = iota((LANES, LANES), 0), iota((LANES, LANES), 1)
    d = k - u
    eye = ones_where((d == 0, 1.0)).astype(BF16)
    for col in range(4):
        rows = [in_ref[c, col, 128:136, :].astype(F32) for c in range(8)]
        rows = jnp.concatenate(rows + [jnp.zeros((64, LANES), F32)]).astype(BF16)
        moved = lax.dot_general(eye, rows, NT, preferred_element_type=F32).astype(BF16)
        for i in range(2):
            edge[i, col * 64 : (col + 1) * 64, :] = moved[i * 64 : (i + 1) * 64]
    slot = u & 7
    used = ((k >> 3) == (u >> 3)) & ((slot == 1) | (slot == 2) | (slot == 5) | (slot == 6))
    grad = ones_where((used & (d == 1), 1.0), (used & (d == -1), -1.0)).astype(BF16)
    for i in range(2):
        values = edge[i]
        grad_img = jnp.dot(values, grad, preferred_element_type=F32)
        summed = tensor_of_cameras(split(values.astype(F32)), split(grad_img))
        for f in range(3):
            for t in range(16):
                edge_sums[f, i, t * 16 : (t + 1) * 16, :] = summed[f][t]

    def values_of(c, i):
        return in_ref[c, :, i * 64 : (i + 1) * 64, :].reshape(256, LANES)

    def gradient(c):
        own = jnp.concatenate([values_of(c, 0), values_of(c, 1)])
        side = jnp.concatenate([edge[0], edge[1]])
        return jnp.dot(
            jnp.concatenate([own, side], axis=1), grads[c], preferred_element_type=F32
        )

    def products(c, grad_img):
        summed = []
        for i in range(2):
            field = split(values_of(c, i).astype(F32))
            for t in range(16):
                scratch[c * 2 + i, t * PITCH : t * PITCH + 16, :] = field[t]
            for r in range(16):
                gray_ref[c * 2 + i, r] = scratch[c * 2 + i, pl.ds(r, 16, stride=PITCH), :]
            summed.append(tensor_of_cameras(field, split(grad_img[i * 256 : (i + 1) * 256])))
        return jnp.concatenate([v for f in range(3) for i in range(2) for v in summed[i][f]])

    def smooth(c, parts):
        for f in range(3):
            own = parts[f * 512 : (f + 1) * 512]
            side = jnp.concatenate([edge_sums[f, 0], edge_sums[f, 1]])
            full = jnp.dot(
                jnp.concatenate([own, side], axis=1), smooths[c], preferred_element_type=F32
            )
            for i in range(2):
                for t in range(16):
                    n = i * 256 + t * 16
                    rows = slice(t * PITCH, t * PITCH + 16)
                    out_ref[f, c * 2 + i, rows, :] = full[n : n + 16]

    grad_img, parts = gradient(0), None
    for c in range(8):
        following = gradient(c + 1) if c < 7 else None
        if c:
            smooth(c - 1, parts)
        parts = products(c, grad_img)
        grad_img = following
    smooth(7, parts)

    for s in range(16):
        smoothers = [Smoother() for _ in range(3)]
        for r in range(1, 15):
            products = products_of(lambda s, r: gray_ref[s, r], s, r)
            for f in range(3):
                value = smoothers[f].push(products[f])
                if r >= 5:
                    sums[f, s, r - 5] = value
    merge_rows(range(3, 13), sums, out_ref, depth_ref)


def parts_of(jaa, jab, jbb, scale):
    spread, total = jaa - jbb, jaa + jbb
    twice = jab + jab
    near = F32(0.1 * scale)
    return spread * spread + twice * twice, total * total + near * F32(scale), jab, jbb + near


def merge(horizontal, vertical):
    nh, dh, bh, ah = parts_of(*horizontal, 1.0)
    nv, dv, bv, av = parts_of(*vertical, 1024.0)
    p, q = nh * dv, nv * dh
    top = p * (bh * av) + q * (bv * ah)
    return top / ((p + q + 0.1 * (dh * dv)) * (ah * av))


def outer_kernel(gray_ref, one_ref, two_ref, hor_ref, inner_ref, out_ref, sums, depth, halo):
    band, last = lax.axis_index("band"), lax.axis_size("band") - 1
    has_low = jnp.where(band > 0, F32(1.0), F32(0.0))
    has_high = jnp.where(band < last, F32(1.0), F32(0.0))

    even = is_even_band()
    for r in range(3):
        for s in range(16):
            one, two = one_ref[r, s].astype(F32), two_ref[r, s].astype(F32)
            halo[r, s] = jnp.where(even, two, one)
            halo[r + 3, s] = jnp.where(even, one, two)

    def field(s, r):
        if r < 0:
            return halo[r + 3, s]
        return gray_ref[s, r] if r < 16 else halo[r - 13, s]

    for s in range(16):
        for side in range(2):
            smoothers = [Smoother() for _ in range(3)]
            for q in range(7):
                r = q + 11 if side else q - 2
                factor = has_low if r < 0 else has_high if r >= 16 else None
                products = products_of(field, s, r, factor)
                for f in range(3):
                    value = smoothers[f].push(products[f])
                    if q >= 4:
                        sums[f, s, side * 3 + q - 4] = value
    merge_rows((0, 1, 2, 13, 14, 15), sums, hor_ref, depth)

    row = iota((16, LANES), 0)
    is_inner = (row >= 3) & (row < 13)
    for s in range(16):
        for t in range(16):
            lines = slice(t * PITCH, t * PITCH + 16)
            value = jnp.where(is_inner, inner_ref[s, lines, :], depth[s, lines, :])
            rows = slice(t % 4 * 16, t % 4 * 16 + 16)
            out_ref[s // 2, t // 4, s % 2, rows, :] = value.astype(BF16)


def spread_kernel(chunks, in_ref, out_ref, scratch, sent):
    copies = []
    for part in range(8):
        rows = slice(part * 16, (part + 1) * 16)
        for chunk in range(chunks):
            scratch[rows, chunk * LANES : (chunk + 1) * LANES] = in_ref[chunk, rows, :].astype(F32)
        copy = pltpu.make_async_copy(scratch.at[rows], out_ref.at[rows], sent.at[part])
        copy.start()
        copies.append(copy)
    for copy in copies:
        copy.wait()


def per_device(light_field, channel_weights):
    group = ("crow", "ccol")
    chunks = lax.axis_size(group)
    bands = lax.axis_size("band")
    params = lambda mib: pltpu.CompilerParams(vmem_limit_bytes=mib * MIB)
    vmem = pl.BlockSpec(memory_space=pltpu.VMEM)
    hbm = pl.BlockSpec(memory_space=pl.ANY)

    packed = pl.pallas_call(
        functools.partial(gray_kernel, chunks),
        in_specs=[hbm, hbm],
        out_specs=hbm,
        out_shape=jax.ShapeDtypeStruct((chunks, 136, LANES), BF16),
        scratch_shapes=[
            pltpu.VMEM((chunks // PIECE, 4, 2, 4, 16, PIECE * LANES), BF16),
            pltpu.VMEM((chunks, 136, LANES), BF16),
            pltpu.SMEM((4,), F32),
            pltpu.SemaphoreType.DMA((chunks // PIECE,)),
            pltpu.SemaphoreType.DMA((chunks // PIECE,)),
            pltpu.SemaphoreType.DMA,
        ],
        compiler_params=params(58),
        name="gray",
    )(channel_weights, light_field)
    columns = lax.all_to_all(packed, group, 0, 0, tiled=True).reshape(8, 4, 136, LANES)
    grads, smooths = pl.pallas_call(
        matrices_kernel,
        out_specs=[vmem, vmem],
        out_shape=[jax.ShapeDtypeStruct((8, 256, LANES), BF16)] * 2,
        compiler_params=params(8),
        cost_estimate=pl.CostEstimate(flops=10**9, bytes_accessed=8 * MIB, transcendentals=0),
        name="matrices",
    )()
    columns, grads, smooths = lax.optimization_barrier((columns, grads, smooths))

    ahead, behind = pl.pallas_call(
        edges_kernel,
        in_specs=[vmem],
        out_specs=[vmem, vmem],
        out_shape=[jax.ShapeDtypeStruct((3, 16, 16, LANES), BF16)] * 2,
        scratch_shapes=[pltpu.VMEM((16, 16 * PITCH, LANES), F32)],
        compiler_params=params(16),
        name="edges",
    )(columns)
    links = [[(n, n + 1) for n in range(start, bands - 1, 2)] for start in range(2)]
    one, two = (
        lax.ppermute(rows, "band", pairs + [(b, a) for a, b in pairs])
        for rows, pairs in zip((ahead, behind), links)
    )

    hor, gray, inner = pl.pallas_call(
        inner_kernel,
        in_specs=[vmem, vmem, vmem],
        out_specs=[vmem, vmem, vmem],
        out_shape=[
            jax.ShapeDtypeStruct((3, 16, 16 * PITCH, LANES), F32),
            jax.ShapeDtypeStruct((16, 16, 16, LANES), F32),
            jax.ShapeDtypeStruct((16, 16 * PITCH, LANES), F32),
        ],
        scratch_shapes=[
            pltpu.VMEM((2, 256, LANES), BF16),
            pltpu.VMEM((3, 2, 256, LANES), BF16),
            pltpu.VMEM((16, 16 * PITCH, LANES), F32),
            pltpu.VMEM((3, 16, 10, 16, LANES), F32),
        ],
        compiler_params=params(28),
        cost_estimate=pl.CostEstimate(flops=10**9, bytes_accessed=8 * MIB, transcendentals=0),
        name="inner",
    )(columns, grads, smooths)

    depth = pl.pallas_call(
        outer_kernel,
        in_specs=[vmem] * 5,
        out_specs=vmem,
        out_shape=jax.ShapeDtypeStruct((8, 4, 2, 64, LANES), BF16),
        scratch_shapes=[
            pltpu.VMEM((3, 16, 6, 16, LANES), F32),
            pltpu.VMEM((16, 16 * PITCH, LANES), F32),
            pltpu.VMEM((6, 16, 16, LANES), F32),
        ],
        compiler_params=params(28),
        name="outer",
    )(gray, one, two, hor, inner)

    back = lax.all_to_all(depth.reshape(chunks, 128, LANES), group, 0, 0, tiled=True)
    out = pl.pallas_call(
        functools.partial(spread_kernel, chunks),
        in_specs=[vmem],
        out_specs=hbm,
        out_shape=jax.ShapeDtypeStruct((128, chunks * LANES), F32),
        scratch_shapes=[pltpu.VMEM((128, chunks * LANES), F32), pltpu.SemaphoreType.DMA((8,))],
        compiler_params=params(8),
        name="spread",
    )(back)
    return out.reshape(2, 4, 16, chunks * LANES)


def solution(mesh):
    placed = (P(None, "crow", "ccol", "band", None), P())
    return jax.shard_map(
        per_device,
        mesh=mesh,
        in_specs=placed,
        out_specs=P("crow", "ccol", "band", None),
        check_vma=False,
    )
```

```python
import functools

import jax
import jax.numpy as jnp
from jax import lax
from jax.experimental import pallas as pl
from jax.experimental.pallas import tpu as pltpu
from jax.sharding import PartitionSpec as P

F32, BF16 = jnp.float32, jnp.bfloat16
LANES = 128
MIB = 1 << 20
NT = (((1,), (1,)), ((), ()))


def iota(shape, dim):
    return lax.broadcasted_iota(jnp.int32, shape, dim)


def ones_where(*conditions_and_values):
    total = None
    for condition, value in conditions_and_values:
        term = jnp.where(condition, F32(value), F32(0.0))
        total = term if total is None else total + term
    return total


PIECE = 8


def gray_kernel(chunks, weights_hbm, field_ref, out_ref, field, packed, weights_ref, arrived, sent, known):
    weights_copy = pltpu.make_async_copy(weights_hbm, weights_ref, known)
    weights_copy.start()
    pieces = chunks // PIECE
    copies = []
    for piece in range(pieces):
        lanes = pl.ds(piece * PIECE * LANES, PIECE * LANES)
        copies.append(
            pltpu.make_async_copy(
                field_ref.at[:, :, :, :, lanes], field.at[piece], arrived.at[piece]
            )
        )
        copies[-1].start()
    row, lane = iota((16, LANES), 0), iota((16, LANES), 1)
    wanted = jnp.where(row < 3, row + 125, jnp.where(row == 3, 0, jnp.where(row == 4, 127, row - 5)))
    select = jnp.where((row < 8) & (lane == wanted), F32(1.0), F32(0.0)).astype(BF16)
    low, middle = row < 3, row < 5
    weights_copy.wait()
    weights = [weights_ref[channel] for channel in range(4)]
    edges = [jnp.zeros((16, LANES), F32)]
    leaving, done = [], 0
    for piece in range(pieces):
        copies[piece].wait()
        for local in range(PIECE):
            chunk = piece * PIECE + local
            lanes = slice(local * LANES, (local + 1) * LANES)
            levels = []
            for cam in range(8):
                total = field[piece, 0, cam // 4, cam % 4, :, lanes].astype(F32) * weights[0]
                for channel in range(1, 4):
                    value = field[piece, channel, cam // 4, cam % 4, :, lanes]
                    total = total + value.astype(F32) * weights[channel]
                levels.append(total.astype(BF16))
            levels = jnp.concatenate(levels)
            packed[chunk, 0:128, :] = levels
            edges.append(lax.dot_general(select, levels, NT, preferred_element_type=F32))
        if piece == pieces - 1:
            edges.append(edges[0])
        ready = len(edges) - 2
        for chunk in range(done, ready):
            left, own, right = edges[chunk : chunk + 3]
            halo = jnp.where(low, left, jnp.where(middle, own, right))
            packed[chunk, 128:136, :] = halo[0:8].astype(BF16)
        part = pl.ds(done, ready - done)
        leaving.append(pltpu.make_async_copy(packed.at[part], out_ref.at[part], sent.at[piece]))
        leaving[-1].start()
        done = ready
    for copy in leaving:
        copy.wait()


PITCH = 17


def is_even_band():
    return lax.rem(lax.axis_index("band"), 2) == 0


def edges_kernel(in_ref, up_ref, down_ref, scratch):
    up = jnp.where(is_even_band(), 13, 0)
    down = 13 - up
    for c in range(8):
        for i in range(2):
            s = c * 2 + i
            for t in range(16):
                rows = slice(i * 64 + t % 4 * 16, i * 64 + t % 4 * 16 + 16)
                scratch[s, t * PITCH : t * PITCH + 16, :] = in_ref[c, t // 4, rows, :].astype(F32)
            for r in range(3):
                up_ref[r, s] = scratch[s, pl.ds(r + up, 16, stride=PITCH), :].astype(BF16)
                down_ref[r, s] = scratch[s, pl.ds(r + down, 16, stride=PITCH), :].astype(BF16)


class Smoother:
    def __init__(self):
        self.last = [None] * 4

    def push(self, value):
        for n in range(4):
            before, self.last[n] = self.last[n], value
            if before is not None:
                value = before if value is None else value + before
        return value


def tensor_of_cameras(field, grad_img):
    count = len(field)
    smoothers = [Smoother() for _ in range(3)]
    result = [[] for _ in range(3)]
    for t in range(count + 2):
        products = (None,) * 3
        if t < count:
            if t == 0:
                grad_cam = -field[1]
            elif t == count - 1:
                grad_cam = field[t - 1]
            else:
                grad_cam = field[t - 1] - field[t + 1]
            products = (grad_cam * grad_cam, grad_cam * grad_img[t], grad_img[t] * grad_img[t])
        for f in range(3):
            value = smoothers[f].push(products[f])
            if t >= 2:
                result[f].append(value.astype(BF16))
    return result


def split(values):
    return [values[n * 16 : (n + 1) * 16] for n in range(values.shape[0] // 16)]


def products_of(field, s, r, factor=None):
    if s == 0:
        grad_cam = -field(1, r)
    elif s == 15:
        grad_cam = field(14, r)
    else:
        grad_cam = field(s - 1, r) - field(s + 1, r)
    grad_img = field(s, r + 1) - field(s, r - 1)
    if factor is not None:
        grad_img = grad_img * factor
    return grad_cam * grad_cam, grad_cam * grad_img, grad_img * grad_img


def merge_rows(rows, sums, hor_ref, depth_ref):
    for n, r in enumerate(rows):
        smoothers = [Smoother() for _ in range(3)]
        lines = pl.ds(r, 16, stride=PITCH)
        for s in range(18):
            vertical = [smoothers[f].push(sums[f, s, n] if s < 16 else None) for f in range(3)]
            if s >= 2:
                horizontal = [hor_ref[f, s - 2, lines, :] for f in range(3)]
                depth_ref[s - 2, lines, :] = merge(horizontal, vertical)


def matrices_kernel(grads, smooths):
    k, u = iota((LANES, LANES), 0), iota((LANES, LANES), 1)
    d = k - u
    dist = jnp.abs(d)
    group = ("crow", "ccol")
    place, last = lax.axis_index(group), lax.axis_size(group) - 1
    unit = 1.0 / 1024.0
    has_left = jnp.where(place > 0, F32(unit), F32(0.0))
    has_right = jnp.where(place < last, F32(unit), F32(0.0))
    h, col = iota((8, LANES), 0), iota((8, LANES), 1)
    grad_edge = ones_where(((h == 2) & (col == 0), -1.0), ((h == 5) & (col == 127), 1.0))
    left = ones_where(
        ((h == 1) & (col == 0), 1.0), ((h == 2) & (col == 0), 4.0), ((h == 2) & (col == 1), 1.0)
    )
    right = ones_where(
        ((h == 5) & (col == 127), 4.0),
        ((h == 5) & (col == 126), 1.0),
        ((h == 6) & (col == 127), 1.0),
    )
    smooth_edge = left * has_left + right * has_right
    grad_own = ones_where((d == 1, 1.0), (d == -1, -1.0)).astype(BF16)
    smooth_own = ones_where(
        (dist == 0, 6.0 * unit), (dist == 1, 4.0 * unit), (dist == 2, unit)
    ).astype(BF16)
    zero = jnp.zeros((8, LANES), F32)
    for c in range(8):
        for matrix, own, side in ((grads, grad_own, grad_edge), (smooths, smooth_own, smooth_edge)):
            matrix[c, 0:128, :] = own
            for n in range(8):
                pair = [side if n * 2 + m == c else zero for m in range(2)]
                matrix[c, 128 + n * 16 : 144 + n * 16, :] = jnp.concatenate(pair).astype(BF16)


def inner_kernel(
    in_ref, grads, smooths, out_ref, gray_ref, depth_ref, edge, edge_sums, scratch, sums
):
    k, u = iota((LANES, LANES), 0), iota((LANES, LANES), 1)
    d = k - u
    eye = ones_where((d == 0, 1.0)).astype(BF16)
    for col in range(4):
        rows = [in_ref[c, col, 128:136, :].astype(F32) for c in range(8)]
        rows = jnp.concatenate(rows + [jnp.zeros((64, LANES), F32)]).astype(BF16)
        moved = lax.dot_general(eye, rows, NT, preferred_element_type=F32).astype(BF16)
        for i in range(2):
            edge[i, col * 64 : (col + 1) * 64, :] = moved[i * 64 : (i + 1) * 64]
    slot = u & 7
    used = ((k >> 3) == (u >> 3)) & ((slot == 1) | (slot == 2) | (slot == 5) | (slot == 6))
    grad = ones_where((used & (d == 1), 1.0), (used & (d == -1), -1.0)).astype(BF16)
    for i in range(2):
        values = edge[i]
        grad_img = jnp.dot(values, grad, preferred_element_type=F32)
        summed = tensor_of_cameras(split(values.astype(F32)), split(grad_img))
        for f in range(3):
            for t in range(16):
                edge_sums[f, i, t * 16 : (t + 1) * 16, :] = summed[f][t]

    def values_of(c, i):
        return in_ref[c, :, i * 64 : (i + 1) * 64, :].reshape(256, LANES)

    def gradient(c):
        own = jnp.concatenate([values_of(c, 0), values_of(c, 1)])
        side = jnp.concatenate([edge[0], edge[1]])
        return jnp.dot(
            jnp.concatenate([own, side], axis=1), grads[c], preferred_element_type=F32
        )

    def products(c, grad_img):
        summed = []
        for i in range(2):
            field = split(values_of(c, i).astype(F32))
            for t in range(16):
                scratch[c * 2 + i, t * PITCH : t * PITCH + 16, :] = field[t]
            for r in range(16):
                gray_ref[c * 2 + i, r] = scratch[c * 2 + i, pl.ds(r, 16, stride=PITCH), :]
            summed.append(tensor_of_cameras(field, split(grad_img[i * 256 : (i + 1) * 256])))
        return jnp.concatenate([v for f in range(3) for i in range(2) for v in summed[i][f]])

    def smooth(c, parts):
        for f in range(3):
            own = parts[f * 512 : (f + 1) * 512]
            side = jnp.concatenate([edge_sums[f, 0], edge_sums[f, 1]])
            full = jnp.dot(
                jnp.concatenate([own, side], axis=1), smooths[c], preferred_element_type=F32
            )
            for i in range(2):
                for t in range(16):
                    n = i * 256 + t * 16
                    rows = slice(t * PITCH, t * PITCH + 16)
                    out_ref[f, c * 2 + i, rows, :] = full[n : n + 16]

    grad_img, parts = gradient(0), None
    for c in range(8):
        following = gradient(c + 1) if c < 7 else None
        if c:
            smooth(c - 1, parts)
        parts = products(c, grad_img)
        grad_img = following
    smooth(7, parts)

    for s in range(16):
        smoothers = [Smoother() for _ in range(3)]
        for r in range(1, 15):
            products = products_of(lambda s, r: gray_ref[s, r], s, r)
            for f in range(3):
                value = smoothers[f].push(products[f])
                if r >= 5:
                    sums[f, s, r - 5] = value
    merge_rows(range(3, 13), sums, out_ref, depth_ref)


def parts_of(jaa, jab, jbb, scale):
    spread, total = jaa - jbb, jaa + jbb
    twice = jab + jab
    near = F32(0.1 * scale)
    return spread * spread + twice * twice, total * total + near * F32(scale), jab, jbb + near


def merge(horizontal, vertical):
    nh, dh, bh, ah = parts_of(*horizontal, 1.0)
    nv, dv, bv, av = parts_of(*vertical, 1024.0)
    p, q = nh * dv, nv * dh
    top = p * (bh * av) + q * (bv * ah)
    return top / ((p + q + 0.1 * (dh * dv)) * (ah * av))


def outer_kernel(gray_ref, one_ref, two_ref, hor_ref, inner_ref, out_ref, sums, depth, halo):
    band, last = lax.axis_index("band"), lax.axis_size("band") - 1
    has_low = jnp.where(band > 0, F32(1.0), F32(0.0))
    has_high = jnp.where(band < last, F32(1.0), F32(0.0))

    even = is_even_band()
    for r in range(3):
        for s in range(16):
            one, two = one_ref[r, s].astype(F32), two_ref[r, s].astype(F32)
            halo[r, s] = jnp.where(even, two, one)
            halo[r + 3, s] = jnp.where(even, one, two)

    def field(s, r):
        if r < 0:
            return halo[r + 3, s]
        return gray_ref[s, r] if r < 16 else halo[r - 13, s]

    for s in range(16):
        for side in range(2):
            smoothers = [Smoother() for _ in range(3)]
            for q in range(7):
                r = q + 11 if side else q - 2
                factor = has_low if r < 0 else has_high if r >= 16 else None
                products = products_of(field, s, r, factor)
                for f in range(3):
                    value = smoothers[f].push(products[f])
                    if q >= 4:
                        sums[f, s, side * 3 + q - 4] = value
    merge_rows((0, 1, 2, 13, 14, 15), sums, hor_ref, depth)

    row = iota((16, LANES), 0)
    is_inner = (row >= 3) & (row < 13)
    for s in range(16):
        for t in range(16):
            lines = slice(t * PITCH, t * PITCH + 16)
            value = jnp.where(is_inner, inner_ref[s, lines, :], depth[s, lines, :])
            rows = slice(t % 4 * 16, t % 4 * 16 + 16)
            out_ref[s // 2, t // 4, s % 2, rows, :] = value.astype(BF16)


def spread_kernel(chunks, in_ref, out_ref, scratch, sent):
    copies = []
    for part in range(8):
        rows = slice(part * 16, (part + 1) * 16)
        for chunk in range(chunks):
            scratch[rows, chunk * LANES : (chunk + 1) * LANES] = in_ref[chunk, rows, :].astype(F32)
        copy = pltpu.make_async_copy(scratch.at[rows], out_ref.at[rows], sent.at[part])
        copy.start()
        copies.append(copy)
    for copy in copies:
        copy.wait()


def per_device(light_field, channel_weights):
    group = ("crow", "ccol")
    chunks = lax.axis_size(group)
    bands = lax.axis_size("band")
    params = lambda mib: pltpu.CompilerParams(vmem_limit_bytes=mib * MIB)
    vmem = pl.BlockSpec(memory_space=pltpu.VMEM)
    hbm = pl.BlockSpec(memory_space=pl.ANY)

    packed = pl.pallas_call(
        functools.partial(gray_kernel, chunks),
        in_specs=[hbm, hbm],
        out_specs=hbm,
        out_shape=jax.ShapeDtypeStruct((chunks, 136, LANES), BF16),
        scratch_shapes=[
            pltpu.VMEM((chunks // PIECE, 4, 2, 4, 16, PIECE * LANES), BF16),
            pltpu.VMEM((chunks, 136, LANES), BF16),
            pltpu.SMEM((4,), F32),
            pltpu.SemaphoreType.DMA((chunks // PIECE,)),
            pltpu.SemaphoreType.DMA((chunks // PIECE,)),
            pltpu.SemaphoreType.DMA,
        ],
        compiler_params=params(58),
        name="gray",
    )(channel_weights, light_field)
    columns = lax.all_to_all(packed, group, 0, 0, tiled=True).reshape(8, 4, 136, LANES)
    grads, smooths = pl.pallas_call(
        matrices_kernel,
        out_specs=[vmem, vmem],
        out_shape=[jax.ShapeDtypeStruct((8, 256, LANES), BF16)] * 2,
        compiler_params=params(8),
        cost_estimate=pl.CostEstimate(flops=10**9, bytes_accessed=8 * MIB, transcendentals=0),
        name="matrices",
    )()
    columns, grads, smooths = lax.optimization_barrier((columns, grads, smooths))

    ahead, behind = pl.pallas_call(
        edges_kernel,
        in_specs=[vmem],
        out_specs=[vmem, vmem],
        out_shape=[jax.ShapeDtypeStruct((3, 16, 16, LANES), BF16)] * 2,
        scratch_shapes=[pltpu.VMEM((16, 16 * PITCH, LANES), F32)],
        compiler_params=params(16),
        name="edges",
    )(columns)
    links = [[(n, n + 1) for n in range(start, bands - 1, 2)] for start in range(2)]
    one, two = (
        lax.ppermute(rows, "band", pairs + [(b, a) for a, b in pairs])
        for rows, pairs in zip((ahead, behind), links)
    )

    hor, gray, inner = pl.pallas_call(
        inner_kernel,
        in_specs=[vmem, vmem, vmem],
        out_specs=[vmem, vmem, vmem],
        out_shape=[
            jax.ShapeDtypeStruct((3, 16, 16 * PITCH, LANES), F32),
            jax.ShapeDtypeStruct((16, 16, 16, LANES), F32),
            jax.ShapeDtypeStruct((16, 16 * PITCH, LANES), F32),
        ],
        scratch_shapes=[
            pltpu.VMEM((2, 256, LANES), BF16),
            pltpu.VMEM((3, 2, 256, LANES), BF16),
            pltpu.VMEM((16, 16 * PITCH, LANES), F32),
            pltpu.VMEM((3, 16, 10, 16, LANES), F32),
        ],
        compiler_params=params(28),
        cost_estimate=pl.CostEstimate(flops=10**9, bytes_accessed=8 * MIB, transcendentals=0),
        name="inner",
    )(columns, grads, smooths)

    depth = pl.pallas_call(
        outer_kernel,
        in_specs=[vmem] * 5,
        out_specs=vmem,
        out_shape=jax.ShapeDtypeStruct((8, 4, 2, 64, LANES), BF16),
        scratch_shapes=[
            pltpu.VMEM((3, 16, 6, 16, LANES), F32),
            pltpu.VMEM((16, 16 * PITCH, LANES), F32),
            pltpu.VMEM((6, 16, 16, LANES), F32),
        ],
        compiler_params=params(28),
        name="outer",
    )(gray, one, two, hor, inner)

    back = lax.all_to_all(depth.reshape(chunks, 128, LANES), group, 0, 0, tiled=True)
    out = pl.pallas_call(
        functools.partial(spread_kernel, chunks),
        in_specs=[vmem],
        out_specs=hbm,
        out_shape=jax.ShapeDtypeStruct((128, chunks * LANES), F32),
        scratch_shapes=[pltpu.VMEM((128, chunks * LANES), F32), pltpu.SemaphoreType.DMA((8,))],
        compiler_params=params(8),
        name="spread",
    )(back)
    return out.reshape(2, 4, 16, chunks * LANES)


def solution(mesh):
    placed = (P(None, "crow", "ccol", "band", None), P())
    return jax.shard_map(
        per_device,
        mesh=mesh,
        in_specs=placed,
        out_specs=P("crow", "ccol", "band", None),
        check_vma=False,
    )
```
